512 devices in a mesh: lon: 128 (over z, x, y_lo), lev: 4 (over y_hi, core).
Axes of the slice: x: 4, y: 4 (y_hi: 2, y_lo: 2; y = y_hi * 2 + y_lo), z: 16, core: 2. Of those that a mesh axis runs over, the one named last changes fastest.
Arguments:
- fields: bfloat16 [16, 8, 2048, 384], P('lev', None, 'lon'), may hold values from -6 to 6
- counts: int32 [8], replicated, may hold values from 2033 to 2048, as said below
- shifts: int32 [2], replicated, may hold values from 0 to 15, as said below
- norm_gains: float32 [3, 384], replicated, may hold values from 0.5 to 1.5
- window_qkv: bfloat16 [3, 384, 384], replicated
- window_out: bfloat16 [384, 384], replicated, may hold values from -0.3125 to 0.3125
- column_qkv: bfloat16 [3, 384, 384], replicated
- column_out: bfloat16 [384, 384], replicated, may hold values from -0.3125 to 0.3125
- mlp_in: bfloat16 [384, 768], replicated, may hold values from -0.3125 to 0.3125
- mlp_out: bfloat16 [768, 384], replicated, may hold values from -0.21875 to 0.21875
Outputs:
- block_out: bfloat16 [16, 8, 2048, 384], P('lev', None, 'lon')
The draws below stay inside these ranges and needn't reach their ends.
Inputs may be any that keep to these rules, and one draw needn't show every extreme that they name: Cells 0 to counts[r] - 1 of row r are real, the others padding; some row has all 2048 real and some row exactly 2033. `shifts`: some block of rows has the offset 16 - 1.
All inputs are finite; a program needn't handle non-finite values.
Results may differ from the reference program's by a relative error of at most 0.015.
Values may be sent and summed in bfloat16 or wider, within the bound.
No kernel may reach another device: no remote copies, remote signals or barrier semaphores. Data moves between devices by JAX's collectives and lax.ppermute only.
A program may use at most 64 MiB of HBM per device.

```python
import math
import jax
import jax.numpy as jnp
from jax import lax

W = 384
HEADS = 12
HID = 768
LEVELS = 16
ROWS = 8
WIN_ROWS = 4
WIN_LON = 16
CELLS = 2048


def draw_counts(key, part):
    key = jax.random.fold_in(key, 3)
    missing = jax.random.randint(key, (ROWS,), 0, WIN_LON)
    lowest = jnp.min(missing)
    highest = jnp.max(missing)
    missing = (missing - lowest) * (WIN_LON - 1) // jnp.maximum(highest - lowest, 1)
    return (CELLS - missing).astype(jnp.int32)


def draw_shifts(key, part):
    key = jax.random.fold_in(key, 5)
    first_key, second_key = jax.random.split(key)
    blocks = ROWS // WIN_ROWS
    offsets = jax.random.randint(first_key, (blocks,), 0, WIN_LON)
    chosen = jax.random.randint(second_key, (), 0, blocks)
    offsets = jnp.where(jnp.arange(blocks) == chosen, WIN_LON - 1, offsets)
    return offsets.astype(jnp.int32)


def draw_window_qkv(key, part):
    key = jax.random.fold_in(key, 11)
    first_key = jax.random.fold_in(key, 0)
    base = jax.random.normal(first_key, (3, W, W), jnp.float32) / math.sqrt(W)
    return base.astype(jnp.bfloat16)


def draw_column_qkv(key, part):
    key = jax.random.fold_in(key, 13)
    first_key = jax.random.fold_in(key, 0)
    base = jax.random.normal(first_key, (3, W, W), jnp.float32) / math.sqrt(W)
    return base.astype(jnp.bfloat16)


def level_of(rng, dims, shards, low, high):
    level = 1.0
    for dim, parts in shards:
        steps = jax.random.uniform(jax.random.fold_in(jax.random.fold_in(rng, 6), dim), (parts,), jnp.float32, low / len(shards), high / len(shards))
        level = level * jnp.repeat(jnp.exp(steps), dims[dim] // parts).reshape((-1,) + (1,) * (len(dims) - 1 - dim))
    return level


def normal_values(key, shape, width, most, cuts=(), kind=jnp.bfloat16):
    values = jax.random.normal(key, shape, jnp.float32) * width
    if len(cuts) > 0:
        values = level_of(key, shape, cuts, -0.22, 0.18) * values
    return jnp.clip(values, min=-most, max=most).astype(kind)


def setup_inputs(seed: int = 0) -> dict:
    arg_keys = jax.random.split(jax.random.key(seed), 11)
    fields = normal_values(arg_keys[0], (LEVELS, ROWS, CELLS, W), 1.0, 6.0, ((0, 4), (2, 128)))
    counts = draw_counts(jax.random.fold_in(arg_keys[10], 71), 0)
    shifts = draw_shifts(jax.random.fold_in(arg_keys[10], 71), 0)
    norm_gains = jnp.clip(1.0 + 0.1 * jax.random.normal(arg_keys[3], (3, W), jnp.float32), 0.5, 1.5)
    window_qkv = draw_window_qkv(jax.random.fold_in(arg_keys[10], 71), 0)
    window_out = normal_values(arg_keys[5], (W, W), W ** -0.5, 0.3125)
    column_qkv = draw_column_qkv(jax.random.fold_in(arg_keys[10], 71), 0)
    column_out = normal_values(arg_keys[7], (W, W), W ** -0.5, 0.3125)
    mlp_in = normal_values(arg_keys[8], (W, HID), W ** -0.5, 0.3125)
    mlp_out = normal_values(arg_keys[9], (HID, W), HID ** -0.5, 0.21875)
    return {"fields": fields, "counts": counts, "shifts": shifts, "norm_gains": norm_gains, "window_qkv": window_qkv, "window_out": window_out, "column_qkv": column_qkv, "column_out": column_out, "mlp_in": mlp_in, "mlp_out": mlp_out}


EPSILON = 1e-05

def layer_norm(values, gain_row):
    values = values.astype(jnp.float32)
    average = lax.optimization_barrier(jnp.mean(values, axis=-1, keepdims=True))
    centred = values - average
    variance = lax.optimization_barrier(jnp.mean(centred * centred, axis=-1, keepdims=True))
    return (centred * lax.rsqrt(variance + EPSILON) * gain_row).astype(jnp.bfloat16)

def softmax_rows(scores):
    highest = lax.optimization_barrier(jnp.max(scores, axis=-1, keepdims=True))
    weights = jnp.exp(scores - highest)
    return (weights / lax.optimization_barrier(jnp.sum(weights, axis=-1, keepdims=True))).astype(jnp.bfloat16)

def window_attend(queries, keys_in, values_in, key_valid):
    level_count, row_count, cell_count, model_width = queries.shape
    head_size = model_width // HEADS
    windows = cell_count // WIN_LON

    def to_windows(tensor):
        tensor = tensor.reshape(level_count, row_count, windows, WIN_LON, HEADS, head_size)
        tensor = tensor.transpose(0, 2, 4, 1, 3, 5)
        return tensor.reshape(level_count, windows, HEADS, row_count * WIN_LON, head_size).astype(jnp.float32)
    scores = jnp.einsum('lnhqd,lnhkd->lnhqk', to_windows(queries), to_windows(keys_in)) / math.sqrt(head_size)
    allowed = key_valid.reshape(row_count, windows, WIN_LON).transpose(1, 0, 2).reshape(windows, row_count * WIN_LON)
    scores = jnp.where(allowed[None, :, None, None, :], scores, -jnp.inf)
    weights_bf = softmax_rows(scores)
    combined = jnp.einsum('lnhqk,lnhkd->lnhqd', weights_bf.astype(jnp.float32), to_windows(values_in)).astype(jnp.bfloat16)
    combined = combined.reshape(level_count, windows, HEADS, row_count, WIN_LON, head_size).transpose(0, 3, 1, 4, 2, 5)
    return combined.reshape(level_count, row_count, cell_count, model_width)

def column_finish(resident, queries, keys_in, values_in, norm_gains, column_out, mlp_in, mlp_out):
    query_levels, columns, model_width = queries.shape
    head_size = model_width // HEADS
    split_q = queries.reshape(query_levels, columns, HEADS, head_size).astype(jnp.float32)
    split_k = keys_in.reshape(keys_in.shape[0], columns, HEADS, head_size).astype(jnp.float32)
    split_v = values_in.reshape(values_in.shape[0], columns, HEADS, head_size).astype(jnp.float32)
    scores = jnp.einsum('qnhd,knhd->nhqk', split_q, split_k) / math.sqrt(head_size)
    weights_bf = softmax_rows(scores)
    combined = jnp.einsum('nhqk,knhd->qnhd', weights_bf.astype(jnp.float32), split_v).astype(jnp.bfloat16)
    combined = combined.reshape(-1, model_width)
    updated = resident.reshape(-1, model_width).astype(jnp.float32) + jnp.dot(combined, column_out, preferred_element_type=jnp.float32)
    updated = updated.astype(jnp.bfloat16)
    normed = layer_norm(updated, norm_gains[2])
    inner_act = jax.nn.gelu(jnp.dot(normed, mlp_in, preferred_element_type=jnp.float32)).astype(jnp.bfloat16)
    result = updated.astype(jnp.float32) + jnp.dot(inner_act, mlp_out, preferred_element_type=jnp.float32)
    return result.astype(jnp.bfloat16).reshape(query_levels, columns, model_width)

def reference(fields, counts, shifts, norm_gains, window_qkv, window_out, column_qkv, column_out, mlp_in, mlp_out):
    level_count, row_count, cell_count, model_width = fields.shape
    cell_ids = jnp.arange(cell_count, dtype=jnp.int32)
    live_cells = cell_ids[None, :] < counts[:, None]

    def one_level(level_field):
        normed = layer_norm(level_field, norm_gains[0]).reshape(-1, model_width)
        triple = [jnp.dot(normed, window_qkv[member], preferred_element_type=jnp.float32).astype(jnp.bfloat16).reshape(row_count, cell_count, model_width) for member in range(3)]
        pieces = []
        for row_block in range(row_count // WIN_ROWS):
            first_row = row_block * WIN_ROWS
            offset = shifts[row_block]
            rolled = [jnp.roll(tensor[first_row:first_row + WIN_ROWS], -offset, axis=1)[None] for tensor in triple]
            rolled_valid = jnp.roll(live_cells[first_row:first_row + WIN_ROWS], -offset, axis=1)
            combined = window_attend(rolled[0], rolled[1], rolled[2], rolled_valid)[0]
            pieces.append(jnp.roll(combined, offset, axis=1))
        attended = jnp.concatenate(pieces, axis=0).reshape(-1, model_width)
        updated = level_field.reshape(-1, model_width).astype(jnp.float32) + jnp.dot(attended, window_out, preferred_element_type=jnp.float32)
        return updated.astype(jnp.bfloat16).reshape(row_count, cell_count, model_width)
    resident = lax.map(one_level, fields)

    def one_row(row_field):
        normed = layer_norm(row_field, norm_gains[1]).reshape(-1, model_width)
        triple = [jnp.dot(normed, column_qkv[member], preferred_element_type=jnp.float32).astype(jnp.bfloat16).reshape(level_count, cell_count, model_width) for member in range(3)]
        return column_finish(row_field, triple[0], triple[1], triple[2], norm_gains, column_out, mlp_in, mlp_out)
    layer_out = lax.map(one_row, resident.transpose(1, 0, 2, 3)).transpose(1, 0, 2, 3)
    return jnp.where(live_cells[None, :, :, None], layer_out, jnp.zeros((), jnp.bfloat16))
```

```python
import functools
import math

import jax
import jax.numpy as jnp
from jax import lax
from jax.experimental import pallas as pl
from jax.experimental.pallas import tpu as pltpu
from jax.sharding import PartitionSpec as P

HEADS = 12
WIN_ROWS = 4
WIN_LON = 16
EPSILON = 1e-05
LANES = 128
F32 = jnp.float32
BF16 = jnp.bfloat16


def move(value, axis, steps):
    count = lax.axis_size(axis)
    pairs = [(source, (source + steps) % count) for source in range(count)]
    return lax.ppermute(value, axis, pairs)


def layer_norm(values, gain_row):
    average = jnp.mean(values, axis=-1, keepdims=True)
    centred = values - average
    variance = jnp.mean(centred * centred, axis=-1, keepdims=True)
    return (centred * lax.rsqrt(variance + EPSILON) * gain_row).astype(BF16)


def dot32(left, right):
    return jnp.dot(left, right, preferred_element_type=F32)


def attend(queries, keys, values, allowed, head_size):
    count, width = queries.shape
    per = LANES // head_size
    scale = math.log2(math.e) / math.sqrt(head_size)
    head_of_lane = lax.broadcasted_iota(jnp.int32, (count, LANES), 1) // head_size
    ones = jnp.ones((keys.shape[0], LANES), BF16)
    pieces = []
    for group in range(width // LANES):
        at = slice(group * LANES, (group + 1) * LANES)
        part = queries[:, at]
        spread = jnp.concatenate(
            [jnp.where(head_of_lane == head, part, jnp.zeros_like(part)) for head in range(per)],
            axis=0,
        )
        scores = lax.dot_general(
            spread, keys[:, at], (((1,), (1,)), ((), ())), preferred_element_type=F32
        ).reshape(per, count, -1)
        scores = jnp.where(allowed[None], scores, -jnp.inf)
        highest = jnp.max(scores, axis=-1, keepdims=True)
        weights = jnp.exp2((scores - highest) * scale).astype(BF16).reshape(per * count, -1)
        mixed = dot32(weights, jnp.concatenate([values[:, at], ones], axis=1))
        mixed = mixed.reshape(per, count, 2 * LANES)
        picked = mixed[0]
        both = jnp.concatenate([head_of_lane, head_of_lane], axis=1)
        for head in range(1, per):
            picked = jnp.where(both == head, mixed[head], picked)
        pieces.append((picked[:, :LANES] / picked[:, LANES:]).astype(BF16))
    return jnp.concatenate(pieces, axis=1)


def count_of_row(counts_ref, first_row, rows):
    wanted = jnp.full(rows.shape, counts_ref[first_row], jnp.int32)
    for row in range(1, WIN_ROWS):
        wanted = jnp.where(rows == row, counts_ref[first_row + row], wanted)
    return wanted


def edge_block(shifts_ref):
    return jnp.where(shifts_ref[0] == WIN_LON - 1, 0, 1)


def window_edge_kernel(
    circle, shifts_ref, counts_ref, anchor_ref, fields_ref, cell_ref, gains_ref, qkv_ref, out_w_ref, result_ref
):
    levels, _, tokens, width = fields_ref.shape
    block = edge_block(shifts_ref)
    anchor = anchor_ref[0]
    own = fields_ref[:, block].reshape(levels * tokens, width).astype(F32)
    cells = cell_ref[...].astype(F32)
    behind = jnp.concatenate(
        [jnp.broadcast_to(cells[n : n + 1], (WIN_LON, width)) for n in range(levels * WIN_ROWS)], axis=0
    )
    place = lax.broadcasted_iota(jnp.int32, own.shape, 0) % WIN_LON
    own = jnp.where(place == WIN_LON - 1, behind, own)
    normed = layer_norm(own, gains_ref[0:1])
    queries, keys, values = [dot32(normed, qkv_ref[n]).astype(BF16) for n in range(3)]

    key = lax.broadcasted_iota(jnp.int32, (tokens, tokens), 1)
    where = key % WIN_LON
    cell = jnp.where(where == WIN_LON - 1, lax.rem(anchor + circle - 1, circle), anchor + where)
    allowed = cell < count_of_row(counts_ref, block * WIN_ROWS, key // WIN_LON)
    mixed = []
    for level in range(levels):
        at = slice(level * tokens, (level + 1) * tokens)
        mixed.append(attend(queries[at], keys[at], values[at], allowed, width // HEADS))
    mixed = jnp.concatenate(mixed, axis=0)
    result_ref[...] = (own + dot32(mixed, out_w_ref[...])).astype(BF16)


def window_both_kernel(
    circle, shifts_ref, counts_ref, anchor_ref, fields_ref, behind_ref, ahead_ref, gains_ref, qkv_ref, out_w_ref,
    result_ref,
):
    levels, _, tokens, width = fields_ref.shape
    block = 1 - edge_block(shifts_ref)
    shift = shifts_ref[block]
    anchor = anchor_ref[0]
    own = fields_ref[:, block].reshape(levels * tokens, width).astype(F32)
    place = lax.broadcasted_iota(jnp.int32, own.shape, 0) % WIN_LON
    other = jnp.where(place < shift, ahead_ref[...].astype(F32), behind_ref[...].astype(F32))
    normed_own = layer_norm(own, gains_ref[0:1])
    normed_other = layer_norm(other, gains_ref[0:1])
    queries = dot32(normed_own, qkv_ref[0]).astype(BF16)
    normed = jnp.concatenate(
        [
            part[level * tokens : (level + 1) * tokens]
            for level in range(levels)
            for part in (normed_own, normed_other)
        ],
        axis=0,
    )
    keys, values = [dot32(normed, qkv_ref[n]).astype(BF16) for n in (1, 2)]

    shape = (tokens, 2 * tokens)
    query_place = lax.broadcasted_iota(jnp.int32, shape, 0) % WIN_LON
    key = lax.broadcasted_iota(jnp.int32, shape, 1)
    where = key % WIN_LON
    here = key < tokens
    cell = anchor + where
    away = jnp.where(where < shift, cell + WIN_LON, cell - WIN_LON + circle)
    cell = jnp.where(here, cell, jnp.where(away >= circle, away - circle, away))
    rows = (key // WIN_LON) % WIN_ROWS
    same = (query_place < shift) == (where < shift)
    allowed = (here == same) & (cell < count_of_row(counts_ref, block * WIN_ROWS, rows))
    mixed = []
    for level in range(levels):
        at = slice(level * tokens, (level + 1) * tokens)
        both = slice(2 * level * tokens, 2 * (level + 1) * tokens)
        mixed.append(attend(queries[at], keys[both], values[both], allowed, width // HEADS))
    mixed = jnp.concatenate(mixed, axis=0)
    result_ref[...] = (own + dot32(mixed, out_w_ref[...])).astype(BF16)


def column_block(core_ref, gathered_ref, gains_ref, qkv_ref, out_w_ref, in_ref, mlp_ref, normed_ref):
    _, tokens, width = gathered_ref.shape
    total = gathered_ref.shape[0] * tokens
    mine = core_ref[0] * 2
    resident = gathered_ref[mine].astype(F32)
    normed = layer_norm(gathered_ref[...].reshape(total, width).astype(F32), gains_ref[1:2])
    normed_ref[...] = normed.reshape(normed_ref.shape)
    queries = dot32(normed_ref[mine], qkv_ref[0]).astype(BF16)
    keys, values = [dot32(normed, qkv_ref[n]).astype(BF16) for n in (1, 2)]

    span = WIN_ROWS * WIN_LON
    levels = tokens // span
    all_levels = total // span
    queries = queries.reshape(levels, WIN_ROWS, WIN_LON, width)
    keys = keys.reshape(all_levels, WIN_ROWS, WIN_LON, width)
    values = values.reshape(all_levels, WIN_ROWS, WIN_LON, width)
    shape = (levels * WIN_LON, all_levels * WIN_LON)
    allowed = (
        lax.broadcasted_iota(jnp.int32, shape, 0) % WIN_LON
        == lax.broadcasted_iota(jnp.int32, shape, 1) % WIN_LON
    )
    rows = []
    for row in range(WIN_ROWS):
        mixed = attend(
            queries[:, row].reshape(levels * WIN_LON, width),
            keys[:, row].reshape(all_levels * WIN_LON, width),
            values[:, row].reshape(all_levels * WIN_LON, width),
            allowed,
            width // HEADS,
        )
        rows.append(mixed.reshape(levels, 1, WIN_LON, width))
    mixed = jnp.concatenate(rows, axis=1).reshape(tokens, width)
    updated = (resident + dot32(mixed, out_w_ref[...])).astype(BF16)
    normed = layer_norm(updated.astype(F32), gains_ref[2:3])
    inner = jax.nn.gelu(dot32(normed, in_ref[...])).astype(BF16)
    return (updated.astype(F32) + dot32(inner, mlp_ref[...])).astype(BF16)


def column_edge_kernel(
    core_ref, gathered_ref, gains_ref, qkv_ref, out_w_ref, in_ref, mlp_ref, result_ref, cell_ref, normed_ref
):
    result = column_block(core_ref, gathered_ref, gains_ref, qkv_ref, out_w_ref, in_ref, mlp_ref, normed_ref)
    result_ref[...] = result
    wide = result.astype(F32)
    last = [wide[n * WIN_LON + WIN_LON - 1 : (n + 1) * WIN_LON] for n in range(cell_ref.shape[0])]
    cell_ref[...] = jnp.concatenate(last, axis=0).astype(BF16)


def column_both_kernel(
    core_ref, shifts_ref, counts_ref, anchor_ref, gathered_ref, edge_ref, cell_ref, gains_ref, qkv_ref, out_w_ref,
    in_ref, mlp_ref, result_ref, normed_ref,
):
    levels, _, tokens, width = result_ref.shape
    block = edge_block(shifts_ref)
    anchor = anchor_ref[0]
    shape = (tokens, width)
    token = lax.broadcasted_iota(jnp.int32, shape, 0)
    place = token % WIN_LON
    edge = edge_ref[...].astype(F32)
    cells = cell_ref[...].astype(F32)
    result = column_block(core_ref, gathered_ref, gains_ref, qkv_ref, out_w_ref, in_ref, mlp_ref, normed_ref)
    result = result.astype(F32)
    live_edge = anchor + place < count_of_row(counts_ref, block * WIN_ROWS, token // WIN_LON)
    live = anchor + place < count_of_row(counts_ref, (1 - block) * WIN_ROWS, token // WIN_LON)
    for level in range(levels):
        at = slice(level * tokens, (level + 1) * tokens)
        last = jnp.concatenate(
            [
                jnp.broadcast_to(cells[n : n + 1], (WIN_LON, width))
                for n in range(level * WIN_ROWS, (level + 1) * WIN_ROWS)
            ],
            axis=0,
        )
        merged = jnp.where(place == WIN_LON - 1, last, edge[at])
        result_ref[level, block] = jnp.where(live_edge, merged, 0.0).astype(BF16)
        result_ref[level, 1 - block] = jnp.where(live, result[at], 0.0).astype(BF16)


def call(body, outs, scalars, arrays, flops, scratch=()):
    smem = pl.BlockSpec(memory_space=pltpu.SMEM)
    vmem = pl.BlockSpec(memory_space=pltpu.VMEM)
    moved = sum(math.prod(a.shape) * a.dtype.itemsize for a in arrays)
    single = len(outs) == 1
    return pl.pallas_call(
        body,
        out_shape=outs[0] if single else outs,
        in_specs=[smem] * len(scalars) + [vmem] * len(arrays),
        out_specs=vmem if single else [vmem] * len(outs),
        scratch_shapes=scratch,
        compiler_params=pltpu.CompilerParams(vmem_limit_bytes=32 * 1024 * 1024),
        cost_estimate=pl.CostEstimate(flops=flops, bytes_accessed=moved, transcendentals=0),
    )(*scalars, *arrays)


def local(
    fields,
    counts,
    shifts,
    norm_gains,
    window_qkv,
    window_out,
    column_qkv,
    column_out,
    mlp_in,
    mlp_out,
):
    levels, row_count, cells, width = fields.shape
    tokens = WIN_ROWS * cells
    circle = cells * lax.axis_size("lon")
    anchor = (lax.axis_index("lon") * cells).astype(jnp.int32).reshape(1)
    core = (lax.axis_index("lev") % 2).astype(jnp.int32).reshape(1)
    blocked = fields.reshape(levels, row_count // WIN_ROWS, WIN_ROWS, cells, width)
    edge = jnp.where(shifts[0] == WIN_LON - 1, 0, 1)
    edge_cells = lax.dynamic_index_in_dim(blocked, edge, 1, keepdims=False)[:, :, cells - 1]
    whole = lax.dynamic_index_in_dim(blocked, 1 - edge, 1, keepdims=False).reshape(-1, width)
    sent_east = jnp.concatenate([edge_cells.reshape(-1, width), whole], axis=0)
    from_behind = move(sent_east, "lon", 1)
    from_ahead = move(whole, "lon", -1)
    cell_count = levels * WIN_ROWS
    behind_cells, behind = from_behind[:cell_count], from_behind[cell_count:]

    blocked = fields.reshape(levels, row_count // WIN_ROWS, tokens, width)
    one = jax.ShapeDtypeStruct((levels * tokens, width), BF16)
    resident_edge = call(
        functools.partial(window_edge_kernel, circle),
        [one],
        [shifts, counts, anchor],
        [blocked, behind_cells, norm_gains, window_qkv, window_out],
        10**9,
    )
    resident_both = call(
        functools.partial(window_both_kernel, circle),
        [one],
        [shifts, counts, anchor],
        [blocked, behind, from_ahead, norm_gains, window_qkv, window_out],
        10**9,
    )

    groups = [[0, 1], [2, 3]]
    swap = [(n, n ^ 2) for n in range(4)]

    def gather(resident):
        other = lax.ppermute(resident, "lev", swap)
        pair = jnp.stack([resident, other])
        return lax.all_gather(pair, "lev", tiled=True, axis_index_groups=groups)

    scratch = [pltpu.VMEM((4, levels * tokens, width), BF16)]
    weights = [norm_gains, column_qkv, column_out, mlp_in, mlp_out]
    edge_result, edge_last = call(
        column_edge_kernel,
        [one, jax.ShapeDtypeStruct((cell_count, width), BF16)],
        [core],
        [gather(resident_edge)] + weights,
        10**9,
        scratch,
    )
    last_cells = move(edge_last, "lon", -1)
    result = call(
        column_both_kernel,
        [jax.ShapeDtypeStruct(blocked.shape, BF16)],
        [core, shifts, counts, anchor],
        [gather(resident_both), edge_result, last_cells] + weights,
        10**9,
        scratch,
    )
    return result.reshape(fields.shape)


def solution(mesh):
    return jax.shard_map(
        local,
        mesh=mesh,
        in_specs=(P("lev", None, "lon", None), P(), P(), P(), P(), P(), P(), P(), P(), P()),
        out_specs=P("lev", None, "lon", None),
        check_vma=False,
    )
```

```python
import functools
import math

import jax
import jax.numpy as jnp
from jax import lax
from jax.experimental import pallas as pl
from jax.experimental.pallas import tpu as pltpu
from jax.sharding import PartitionSpec as P

HEADS = 12
WIN_ROWS = 4
WIN_LON = 16
EPSILON = 1e-05
LANES = 128
CORES = 2
F32 = jnp.float32
BF16 = jnp.bfloat16


def layer_norm(values, gain_row):
    average = jnp.mean(values, axis=-1, keepdims=True)
    centred = values - average
    variance = jnp.mean(centred * centred, axis=-1, keepdims=True)
    return (centred * lax.rsqrt(variance + EPSILON) * gain_row).astype(BF16)


def dot32(left, right):
    return jnp.dot(left, right, preferred_element_type=F32)


def attend(units, allowed, head_size):
    count, width = units[0][0].shape
    per = LANES // head_size
    scale = math.log2(math.e) / math.sqrt(head_size)
    head_of_lane = lax.broadcasted_iota(jnp.int32, (count, LANES), 1) // head_size
    both = jnp.concatenate([head_of_lane, head_of_lane], axis=1)
    ones = jnp.ones((units[0][1].shape[0], LANES), BF16)
    groups = width // LANES
    cuts = [slice(group * LANES, (group + 1) * LANES) for group in range(groups)]
    jobs = [[part[:, at] for part in unit] for unit in units for at in cuts]
    scores = []
    for queries, keys, _ in jobs:
        spread = jnp.concatenate(
            [jnp.where(head_of_lane == head, queries, jnp.zeros_like(queries)) for head in range(per)], axis=0
        )
        scores.append(
            lax.dot_general(spread, keys, (((1,), (1,)), ((), ())), preferred_element_type=F32)
        )
    weights = []
    for score in scores:
        score = jnp.where(allowed[None], score.reshape(per, count, -1), -jnp.inf)
        highest = jnp.max(score, axis=-1, keepdims=True)
        weights.append(jnp.exp2((score - highest) * scale).astype(BF16).reshape(per * count, -1))
    mixes = [
        dot32(weight, jnp.concatenate([values, ones], axis=1)).reshape(per, count, 2 * LANES)
        for weight, (_, _, values) in zip(weights, jobs)
    ]
    pieces = []
    for mixed in mixes:
        picked = mixed[0]
        for head in range(1, per):
            picked = jnp.where(both == head, mixed[head], picked)
        pieces.append((picked[:, :LANES] / picked[:, LANES:]).astype(BF16))
    return [
        jnp.concatenate(pieces[first : first + groups], axis=1) for first in range(0, len(pieces), groups)
    ]


SHIFT, BOTH_COUNTS, EDGE_COUNTS, FACTS = 0, 1, 5, 16


def fact(facts_ref, row):
    return facts_ref[row : row + 1, :1]


def count_of_row(facts_ref, first, rows):
    wanted = fact(facts_ref, first)
    for row in range(1, WIN_ROWS):
        wanted = jnp.where(rows == row, fact(facts_ref, first + row), wanted)
    return wanted


def edge_block(shifts_ref):
    return jnp.where(shifts_ref[0] == WIN_LON - 1, 0, 1)


def pack_kernel(
    shifts_hbm, counts_hbm, fields_hbm, gains_hbm, qkv_hbm, out_w_hbm, east_ref, edge_ref, other_ref, facts_ref,
    gains_ref, qkv_ref, out_w_ref, shifts_ref, counts_ref, fields_ref, sems,
):
    runs, cells, width = edge_ref.shape
    moves = [
        (shifts_hbm, shifts_ref), (counts_hbm, counts_ref), (fields_hbm, fields_ref), (gains_hbm, gains_ref),
        (qkv_hbm, qkv_ref), (out_w_hbm, out_w_ref),
    ]
    copies = [pltpu.make_async_copy(*ends, sems.at[n]) for n, ends in enumerate(moves)]
    for copy in copies:
        copy.start()
    for copy in copies[:3]:
        copy.wait()
    block = edge_block(shifts_ref)
    edge = fields_ref[:, block].reshape(runs, cells, width)
    other = fields_ref[:, 1 - block].reshape(runs, cells, width)
    edge_ref[...] = edge
    other_ref[...] = east_ref[1:] = other
    edge = edge.astype(F32)
    east_ref[0] = jnp.concatenate([edge[run, cells - 1 :] for run in range(runs)], axis=0).astype(BF16)
    numbers = [shifts_ref[1 - block]]
    numbers += [counts_ref[(1 - block) * WIN_ROWS + row] for row in range(WIN_ROWS)]
    numbers += [counts_ref[block * WIN_ROWS + row] for row in range(WIN_ROWS)]
    place = lax.broadcasted_iota(jnp.int32, facts_ref.shape, 0)
    facts = jnp.zeros(facts_ref.shape, jnp.int32)
    for row, number in enumerate(numbers):
        facts = jnp.where(place == row, number, facts)
    facts_ref[...] = facts
    for copy in copies[3:]:
        copy.wait()


def window_block(
    circle, shift, counts_row, other, own, facts_ref, anchor_ref, gains_ref, qkv_ref, out_w_ref, result_ref, normed_ref
):
    total, width = own.shape
    tokens = WIN_ROWS * WIN_LON
    anchor = anchor_ref[:1, :1]
    normed = layer_norm(own, gains_ref[0:1])
    queries = dot32(normed, qkv_ref[0]).astype(BF16)
    other = layer_norm(other, gains_ref[0:1])
    normed = jnp.concatenate(
        [part[first : first + tokens] for first in range(0, total, tokens) for part in (normed, other)], axis=0
    )
    keys, values = [dot32(normed, qkv_ref[n]).astype(BF16) for n in (1, 2)]

    shape = (tokens, 2 * tokens)
    query_place = lax.broadcasted_iota(jnp.int32, shape, 0) % WIN_LON
    key = lax.broadcasted_iota(jnp.int32, shape, 1)
    where = key % WIN_LON
    here = key < tokens
    cell = anchor + where
    away = jnp.where(where < shift, cell + WIN_LON, cell - WIN_LON + circle)
    cell = jnp.where(here, cell, jnp.where(away >= circle, away - circle, away))
    same = (query_place < shift) == (where < shift)
    allowed = (here == same) & (cell < count_of_row(facts_ref, counts_row, (key // WIN_LON) % WIN_ROWS))
    units = []
    for first in range(0, total, tokens):
        both = slice(2 * first, 2 * (first + tokens))
        units.append((queries[first : first + tokens], keys[both], values[both]))
    mixed = attend(units, allowed, width // HEADS)
    resident = (own + dot32(jnp.concatenate(mixed, axis=0), out_w_ref[...])).astype(BF16)
    result_ref[...] = resident
    normed_ref[...] = layer_norm(resident.astype(F32), gains_ref[1:2])


def window_edge_kernel(
    circle, facts_ref, anchor_ref, own_ref, behind_ref, ahead_ref, gains_ref, qkv_ref, out_w_ref, _,
    result_ref, normed_ref,
):
    total, width = result_ref.shape
    cells = behind_ref[0].astype(F32)
    behind = jnp.concatenate(
        [jnp.broadcast_to(cells[n : n + 1], (WIN_LON, width)) for n in range(total // WIN_LON)], axis=0
    )
    place = lax.broadcasted_iota(jnp.int32, (total, width), 0) % WIN_LON
    other = jnp.where(place == WIN_LON - 1, behind, ahead_ref[...].reshape(total, width).astype(F32))
    window_block(
        circle, WIN_LON - 1, EDGE_COUNTS, other, own_ref[...].reshape(total, width).astype(F32), facts_ref,
        anchor_ref, gains_ref, qkv_ref, out_w_ref, result_ref, normed_ref,
    )


def window_both_kernel(
    circle, facts_ref, anchor_ref, own_ref, behind_ref, ahead_ref, gains_ref, qkv_ref, out_w_ref, result_ref,
    normed_ref,
):
    total, width = result_ref.shape
    shift = fact(facts_ref, SHIFT)
    place = lax.broadcasted_iota(jnp.int32, (total, width), 0) % WIN_LON
    behind = behind_ref[1:].reshape(total, width).astype(F32)
    ahead = ahead_ref[...].reshape(total, width).astype(F32)
    window_block(
        circle, shift, BOTH_COUNTS, jnp.where(place < shift, ahead, behind),
        own_ref[...].reshape(total, width).astype(F32), facts_ref, anchor_ref, gains_ref, qkv_ref, out_w_ref,
        result_ref, normed_ref,
    )


def column_attend(normed_ref, gathered_ref, qkv_ref):
    parts, tokens, width = gathered_ref.shape
    total = parts * tokens
    normed = gathered_ref[...].reshape(total, width)
    queries = dot32(normed_ref[...], qkv_ref[0]).astype(BF16)
    keys, values = [dot32(normed, qkv_ref[n]).astype(BF16) for n in (1, 2)]

    span = WIN_ROWS * WIN_LON
    levels = tokens // span
    all_levels = total // span
    queries = queries.reshape(levels, WIN_ROWS, WIN_LON, width)
    keys = keys.reshape(all_levels, WIN_ROWS, WIN_LON, width)
    values = values.reshape(all_levels, WIN_ROWS, WIN_LON, width)
    shape = (levels * WIN_LON, all_levels * WIN_LON)
    allowed = (
        lax.broadcasted_iota(jnp.int32, shape, 0) % WIN_LON
        == lax.broadcasted_iota(jnp.int32, shape, 1) % WIN_LON
    )
    mixed = []
    for first in range(0, WIN_ROWS, 2):
        units = [
            (
                queries[:, row].reshape(levels * WIN_LON, width),
                keys[:, row].reshape(all_levels * WIN_LON, width),
                values[:, row].reshape(all_levels * WIN_LON, width),
            )
            for row in (first, first + 1)
        ]
        mixed += attend(units, allowed, width // HEADS)
    mixed = jnp.concatenate([part.reshape(levels, 1, WIN_LON, width) for part in mixed], axis=1)
    return mixed.reshape(tokens, width)


def feed_forward(mixed, resident_ref, gains_ref, out_w_ref, in_ref, mlp_ref):
    tokens = mixed.shape[0]
    half = tokens // 2
    halves = [slice(0, half), slice(half, tokens)]
    updated = [
        (resident_ref[at].astype(F32) + dot32(mixed[at], out_w_ref[...])).astype(BF16) for at in halves
    ]
    normed = [layer_norm(part.astype(F32), gains_ref[2:3]) for part in updated]
    inner = [dot32(part, in_ref[...]) for part in normed]
    inner = [jax.nn.gelu(part).astype(BF16) for part in inner]
    result = [part.astype(F32) + dot32(act, mlp_ref[...]) for part, act in zip(updated, inner)]
    return jnp.concatenate(result, axis=0)


def live_cells(facts_ref, anchor_ref, counts_row, values):
    tokens = WIN_ROWS * WIN_LON
    width = values.shape[1]
    token = lax.broadcasted_iota(jnp.int32, (tokens, width), 0)
    live = anchor_ref[:1, :1] + token % WIN_LON < count_of_row(facts_ref, counts_row, token // WIN_LON)
    return jnp.where(live[None], values.reshape(-1, tokens, width), 0.0).astype(BF16)


def column_first_kernel(
    facts_ref, anchor_ref, resident_ref, normed_ref, gathered_ref, gains_ref, qkv_ref, out_w_ref, in_ref, mlp_ref,
    result_ref,
):
    mixed = column_attend(normed_ref, gathered_ref, qkv_ref)
    result = feed_forward(mixed, resident_ref, gains_ref, out_w_ref, in_ref, mlp_ref)
    result_ref[...] = live_cells(facts_ref, anchor_ref, BOTH_COUNTS, result)


def column_last_kernel(
    shifts_hbm, facts_ref, anchor_ref, resident_ref, normed_ref, gathered_ref, first_ref, gains_ref, qkv_ref,
    out_w_ref, in_ref, mlp_ref, result_ref, stage_ref, shifts_ref, sems,
):
    shifts_copy = pltpu.make_async_copy(shifts_hbm, shifts_ref, sems.at[2])
    shifts_copy.start()
    mixed = column_attend(normed_ref, gathered_ref, qkv_ref)
    shifts_copy.wait()
    block = edge_block(shifts_ref)
    first = pltpu.make_async_copy(first_ref, result_ref.at[:, 1 - block], sems.at[0])
    first.start()
    result = feed_forward(mixed, resident_ref, gains_ref, out_w_ref, in_ref, mlp_ref)
    stage_ref[...] = live_cells(facts_ref, anchor_ref, EDGE_COUNTS, result)
    second = pltpu.make_async_copy(stage_ref, result_ref.at[:, block], sems.at[1])
    second.start()
    first.wait()
    second.wait()


def call(body, outs, scalars, arrays, flops, scratch=(), spaces=None, out_spaces=None):
    spaces = spaces or [pltpu.VMEM] * len(arrays)
    out = [pl.BlockSpec(memory_space=space) for space in out_spaces or [pltpu.VMEM] * len(outs)]
    moved = sum(math.prod(a.shape) * a.dtype.itemsize for a in arrays)
    single = len(outs) == 1
    arrays = [
        pltpu.with_memory_space_constraint(array, space) if space == pltpu.HBM else array
        for array, space in zip(arrays, spaces)
    ]
    return pl.pallas_call(
        body,
        out_shape=outs[0] if single else outs,
        in_specs=[pl.BlockSpec(memory_space=pltpu.SMEM)] * len(scalars)
        + [pl.BlockSpec(memory_space=space) for space in spaces],
        out_specs=out[0] if single else out,
        scratch_shapes=scratch,
        compiler_params=pltpu.CompilerParams(vmem_limit_bytes=24 * 1024 * 1024),
        cost_estimate=pl.CostEstimate(flops=flops, bytes_accessed=moved, transcendentals=0),
    )(*scalars, *arrays)


def local(
    fields,
    counts,
    shifts,
    norm_gains,
    window_qkv,
    window_out,
    column_qkv,
    column_out,
    mlp_in,
    mlp_out,
):
    levels, row_count, cells, width = fields.shape
    blocks = row_count // WIN_ROWS
    tokens = WIN_ROWS * cells
    total = levels * tokens
    runs = levels * WIN_ROWS
    tiles = lax.axis_size("lon")
    circle = cells * tiles
    anchor = jnp.full((8, LANES), lax.axis_index("lon") * cells, jnp.int32)

    weights = [norm_gains, window_qkv, window_out]
    sent, edge, other, facts, *weights = call(
        pack_kernel,
        [
            jax.ShapeDtypeStruct((1 + runs, cells, width), BF16),
            jax.ShapeDtypeStruct((runs, cells, width), BF16),
            jax.ShapeDtypeStruct((runs, cells, width), BF16),
            jax.ShapeDtypeStruct((FACTS, LANES), jnp.int32),
        ]
        + [jax.ShapeDtypeStruct(array.shape, array.dtype) for array in weights],
        [],
        [shifts, counts, fields.reshape(levels, blocks, WIN_ROWS, cells, width)] + weights,
        10**6,
        [
            pltpu.SMEM(shifts.shape, jnp.int32),
            pltpu.SMEM(counts.shape, jnp.int32),
            pltpu.VMEM((levels, blocks, WIN_ROWS, cells, width), BF16),
            pltpu.SemaphoreType.DMA((6,)),
        ],
        [pltpu.HBM] * 6,
    )
    west = [(tile, (tile - 1) % tiles) for tile in range(tiles)]
    behind = lax.ppermute(sent, "lon", [pair[::-1] for pair in west])
    ahead_other = lax.ppermute(other, "lon", west)

    one = jax.ShapeDtypeStruct((total, width), BF16)
    ahead_edge = lax.ppermute(edge, "lon", west)

    resident_other, normed_other = call(
        functools.partial(window_both_kernel, circle),
        [one, one],
        [],
        [facts, anchor, other, behind, ahead_other] + weights,
        10**9,
    )
    resident_edge, normed_edge = call(
        functools.partial(window_edge_kernel, circle),
        [one, one],
        [],
        [facts, anchor, edge, behind, ahead_edge] + weights + [resident_other],
        10**9,
        spaces=[pltpu.VMEM] * (5 + len(weights)) + [pl.ANY],
    )

    groups = [[first, first + 1] for first in range(0, 2 * CORES, CORES)]
    swap = [(n, n ^ CORES) for n in range(2 * CORES)]

    def gather(part, other):
        return lax.all_gather(jnp.stack([part, other]), "lev", tiled=True, axis_index_groups=groups)

    swapped_other, swapped_edge = [lax.ppermute(part, "lev", swap) for part in (normed_other, normed_edge)]
    weights = [norm_gains, column_qkv, column_out, mlp_in, mlp_out]
    first = call(
        column_first_kernel,
        [jax.ShapeDtypeStruct((levels, tokens, width), BF16)],
        [],
        [facts, anchor, resident_other, normed_other, gather(normed_other, swapped_other)] + weights,
        10**9,
    )
    first, swapped_edge = lax.optimization_barrier((first, swapped_edge))
    result = call(
        column_last_kernel,
        [jax.ShapeDtypeStruct((levels, blocks, tokens, width), BF16)],
        [],
        [shifts, facts, anchor, resident_edge, normed_edge, gather(normed_edge, swapped_edge), first] + weights,
        10**9,
        [
            pltpu.VMEM((levels, tokens, width), BF16),
            pltpu.SMEM(shifts.shape, jnp.int32),
            pltpu.SemaphoreType.DMA((3,)),
        ],
        [pltpu.HBM] + [pltpu.VMEM] * (6 + len(weights)),
        out_spaces=[pltpu.HBM],
    )
    return result.reshape(fields.shape)


def solution(mesh):
    return jax.shard_map(
        local,
        mesh=mesh,
        in_specs=(P("lev", None, "lon", None), P(), P(), P(), P(), P(), P(), P(), P(), P()),
        out_specs=P("lev", None, "lon", None),
        check_vma=False,
    )
```

```python
import functools
import math

import jax
import jax.numpy as jnp
from jax import lax
from jax.experimental import pallas as pl
from jax.experimental.pallas import tpu as pltpu
from jax.sharding import PartitionSpec as P

HEADS = 12
WIN_ROWS = 4
WIN_LON = 16
EPSILON = 1e-05
LANES = 128
CORES = 2
F32 = jnp.float32
BF16 = jnp.bfloat16


def layer_norm(values, gain_row):
    average = jnp.mean(values, axis=-1, keepdims=True)
    centred = values - average
    variance = jnp.mean(centred * centred, axis=-1, keepdims=True)
    return (centred * lax.rsqrt(variance + EPSILON) * gain_row).astype(BF16)


def dot32(left, right):
    return jnp.dot(left, right, preferred_element_type=F32)


def attend(units, allowed, head_size):
    count, width = units[0][0].shape
    per = LANES // head_size
    scale = math.log2(math.e) / math.sqrt(head_size)
    head_of_lane = lax.broadcasted_iota(jnp.int32, (count, LANES), 1) // head_size
    both = jnp.concatenate([head_of_lane, head_of_lane], axis=1)
    ones = jnp.ones((units[0][1].shape[0], LANES), BF16)
    groups = width // LANES
    cuts = [slice(group * LANES, (group + 1) * LANES) for group in range(groups)]
    jobs = [[part[:, at] for part in unit] for unit in units for at in cuts]
    scores = []
    for queries, keys, _ in jobs:
        spread = jnp.concatenate(
            [jnp.where(head_of_lane == head, queries, jnp.zeros_like(queries)) for head in range(per)], axis=0
        )
        scores.append(
            lax.dot_general(spread, keys, (((1,), (1,)), ((), ())), preferred_element_type=F32)
        )
    weights = []
    for score in scores:
        score = jnp.where(allowed[None], score.reshape(per, count, -1), -jnp.inf)
        highest = jnp.max(score, axis=-1, keepdims=True)
        weights.append(jnp.exp2((score - highest) * scale).astype(BF16).reshape(per * count, -1))
    mixes = [
        dot32(weight, jnp.concatenate([values, ones], axis=1)).reshape(per, count, 2 * LANES)
        for weight, (_, _, values) in zip(weights, jobs)
    ]
    pieces = []
    for mixed in mixes:
        picked = mixed[0]
        for head in range(1, per):
            picked = jnp.where(both == head, mixed[head], picked)
        pieces.append((picked[:, :LANES] / picked[:, LANES:]).astype(BF16))
    return [
        jnp.concatenate(pieces[first : first + groups], axis=1) for first in range(0, len(pieces), groups)
    ]


SHIFT, BOTH_COUNTS, EDGE_COUNTS, FACTS = 0, 1, 5, 16


def fact(facts_ref, row):
    return facts_ref[row : row + 1, :1]


def count_of_row(facts_ref, first, rows):
    wanted = fact(facts_ref, first)
    for row in range(1, WIN_ROWS):
        wanted = jnp.where(rows == row, fact(facts_ref, first + row), wanted)
    return wanted


def edge_block(shifts_ref):
    return jnp.where(shifts_ref[0] == WIN_LON - 1, 0, 1)


def pack_kernel(
    shifts_hbm, counts_hbm, fields_hbm, gains_hbm, qkv_hbm, out_w_hbm, east_ref, edge_ref, other_ref, facts_ref,
    gains_ref, qkv_ref, out_w_ref, shifts_ref, counts_ref, fields_ref, sems,
):
    runs, cells, width = edge_ref.shape
    moves = [
        (shifts_hbm, shifts_ref), (counts_hbm, counts_ref), (fields_hbm, fields_ref), (gains_hbm, gains_ref),
        (qkv_hbm, qkv_ref), (out_w_hbm, out_w_ref),
    ]
    copies = [pltpu.make_async_copy(*ends, sems.at[n]) for n, ends in enumerate(moves)]
    for copy in copies:
        copy.start()
    for copy in copies[:3]:
        copy.wait()
    block = edge_block(shifts_ref)
    edge = fields_ref[:, block].reshape(runs, cells, width)
    other = fields_ref[:, 1 - block].reshape(runs, cells, width)
    edge_ref[...] = edge
    other_ref[...] = east_ref[1:] = other
    edge = edge.astype(F32)
    east_ref[0] = jnp.concatenate([edge[run, cells - 1 :] for run in range(runs)], axis=0).astype(BF16)
    numbers = [shifts_ref[1 - block]]
    numbers += [counts_ref[(1 - block) * WIN_ROWS + row] for row in range(WIN_ROWS)]
    numbers += [counts_ref[block * WIN_ROWS + row] for row in range(WIN_ROWS)]
    place = lax.broadcasted_iota(jnp.int32, facts_ref.shape, 0)
    facts = jnp.zeros(facts_ref.shape, jnp.int32)
    for row, number in enumerate(numbers):
        facts = jnp.where(place == row, number, facts)
    facts_ref[...] = facts
    for copy in copies[3:]:
        copy.wait()


def own_kernel(edge_ref, other_ref, gains_ref, qkv_ref, edge_out_ref, other_out_ref):
    total, width = edge_out_ref.shape[1:]
    outs = (edge_out_ref, other_out_ref)
    normed = [
        layer_norm(own[...].reshape(total, width).astype(F32), gains_ref[0:1]) for own in (edge_ref, other_ref)
    ]
    for n in range(3):
        for part, out_ref in zip(normed, outs):
            out_ref[n] = dot32(part, qkv_ref[n]).astype(BF16)


def window_block(
    circle, shift, counts_row, other, own, done_ref, facts_ref, anchor_ref, gains_ref, qkv_ref, out_w_ref, result_ref,
    normed_ref,
):
    total, width = own.shape
    tokens = WIN_ROWS * WIN_LON
    anchor = anchor_ref[:1, :1]
    normed = layer_norm(other, gains_ref[0:1])
    keys, values = [dot32(normed, qkv_ref[n]).astype(BF16) for n in (1, 2)]

    shape = (tokens, 2 * tokens)
    query_place = lax.broadcasted_iota(jnp.int32, shape, 0) % WIN_LON
    key = lax.broadcasted_iota(jnp.int32, shape, 1)
    where = key % WIN_LON
    here = key < tokens
    cell = anchor + where
    away = jnp.where(where < shift, cell + WIN_LON, cell - WIN_LON + circle)
    cell = jnp.where(here, cell, jnp.where(away >= circle, away - circle, away))
    same = (query_place < shift) == (where < shift)
    allowed = (here == same) & (cell < count_of_row(facts_ref, counts_row, (key // WIN_LON) % WIN_ROWS))
    units = []
    for first in range(0, total, tokens):
        at = slice(first, first + tokens)
        units.append(
            (
                done_ref[0, at],
                jnp.concatenate([done_ref[1, at], keys[at]], axis=0),
                jnp.concatenate([done_ref[2, at], values[at]], axis=0),
            )
        )
    mixed = attend(units, allowed, width // HEADS)
    resident = (own + dot32(jnp.concatenate(mixed, axis=0), out_w_ref[...])).astype(BF16)
    result_ref[...] = resident
    normed_ref[...] = layer_norm(resident.astype(F32), gains_ref[1:2])


def window_edge_kernel(
    circle, facts_ref, anchor_ref, own_ref, done_ref, behind_ref, ahead_ref, gains_ref, qkv_ref, out_w_ref, _,
    result_ref, normed_ref,
):
    total, width = result_ref.shape
    cells = behind_ref[0].astype(F32)
    behind = jnp.concatenate(
        [jnp.broadcast_to(cells[n : n + 1], (WIN_LON, width)) for n in range(total // WIN_LON)], axis=0
    )
    place = lax.broadcasted_iota(jnp.int32, (total, width), 0) % WIN_LON
    other = jnp.where(place == WIN_LON - 1, behind, ahead_ref[...].reshape(total, width).astype(F32))
    window_block(
        circle, WIN_LON - 1, EDGE_COUNTS, other, own_ref[...].reshape(total, width).astype(F32), done_ref, facts_ref,
        anchor_ref, gains_ref, qkv_ref, out_w_ref, result_ref, normed_ref,
    )


def window_both_kernel(
    circle, facts_ref, anchor_ref, own_ref, done_ref, behind_ref, ahead_ref, gains_ref, qkv_ref, out_w_ref, result_ref,
    normed_ref,
):
    total, width = result_ref.shape
    shift = fact(facts_ref, SHIFT)
    place = lax.broadcasted_iota(jnp.int32, (total, width), 0) % WIN_LON
    behind = behind_ref[1:].reshape(total, width).astype(F32)
    ahead = ahead_ref[...].reshape(total, width).astype(F32)
    window_block(
        circle, shift, BOTH_COUNTS, jnp.where(place < shift, ahead, behind),
        own_ref[...].reshape(total, width).astype(F32), done_ref, facts_ref, anchor_ref, gains_ref, qkv_ref, out_w_ref,
        result_ref, normed_ref,
    )


def column_attend(normed_ref, gathered_ref, qkv_ref):
    parts, tokens, width = gathered_ref.shape
    total = parts * tokens
    normed = gathered_ref[...].reshape(total, width)
    queries = dot32(normed_ref[...], qkv_ref[0]).astype(BF16)
    keys, values = [dot32(normed, qkv_ref[n]).astype(BF16) for n in (1, 2)]

    span = WIN_ROWS * WIN_LON
    levels = tokens // span
    all_levels = total // span
    queries = queries.reshape(levels, WIN_ROWS, WIN_LON, width)
    keys = keys.reshape(all_levels, WIN_ROWS, WIN_LON, width)
    values = values.reshape(all_levels, WIN_ROWS, WIN_LON, width)
    shape = (levels * WIN_LON, all_levels * WIN_LON)
    allowed = (
        lax.broadcasted_iota(jnp.int32, shape, 0) % WIN_LON
        == lax.broadcasted_iota(jnp.int32, shape, 1) % WIN_LON
    )
    mixed = []
    for first in range(0, WIN_ROWS, 2):
        units = [
            (
                queries[:, row].reshape(levels * WIN_LON, width),
                keys[:, row].reshape(all_levels * WIN_LON, width),
                values[:, row].reshape(all_levels * WIN_LON, width),
            )
            for row in (first, first + 1)
        ]
        mixed += attend(units, allowed, width // HEADS)
    mixed = jnp.concatenate([part.reshape(levels, 1, WIN_LON, width) for part in mixed], axis=1)
    return mixed.reshape(tokens, width)


def feed_forward(mixed, resident_ref, gains_ref, out_w_ref, in_ref, mlp_ref):
    tokens = mixed.shape[0]
    half = tokens // 2
    halves = [slice(0, half), slice(half, tokens)]
    updated = [
        (resident_ref[at].astype(F32) + dot32(mixed[at], out_w_ref[...])).astype(BF16) for at in halves
    ]
    normed = [layer_norm(part.astype(F32), gains_ref[2:3]) for part in updated]
    inner = [dot32(part, in_ref[...]) for part in normed]
    inner = [jax.nn.gelu(part).astype(BF16) for part in inner]
    result = [part.astype(F32) + dot32(act, mlp_ref[...]) for part, act in zip(updated, inner)]
    return jnp.concatenate(result, axis=0)


def live_cells(facts_ref, anchor_ref, counts_row, values):
    tokens = WIN_ROWS * WIN_LON
    width = values.shape[1]
    token = lax.broadcasted_iota(jnp.int32, (tokens, width), 0)
    live = anchor_ref[:1, :1] + token % WIN_LON < count_of_row(facts_ref, counts_row, token // WIN_LON)
    return jnp.where(live[None], values.reshape(-1, tokens, width), 0.0).astype(BF16)


def column_first_kernel(
    facts_ref, anchor_ref, resident_ref, normed_ref, gathered_ref, gains_ref, qkv_ref, out_w_ref, in_ref, mlp_ref,
    result_ref,
):
    mixed = column_attend(normed_ref, gathered_ref, qkv_ref)
    result = feed_forward(mixed, resident_ref, gains_ref, out_w_ref, in_ref, mlp_ref)
    result_ref[...] = live_cells(facts_ref, anchor_ref, BOTH_COUNTS, result)


def column_last_kernel(
    shifts_hbm, facts_ref, anchor_ref, resident_ref, normed_ref, gathered_ref, first_ref, gains_ref, qkv_ref,
    out_w_ref, in_ref, mlp_ref, result_ref, stage_ref, shifts_ref, sems,
):
    shifts_copy = pltpu.make_async_copy(shifts_hbm, shifts_ref, sems.at[2])
    shifts_copy.start()
    mixed = column_attend(normed_ref, gathered_ref, qkv_ref)
    shifts_copy.wait()
    block = edge_block(shifts_ref)
    first = pltpu.make_async_copy(first_ref, result_ref.at[:, 1 - block], sems.at[0])
    first.start()
    result = feed_forward(mixed, resident_ref, gains_ref, out_w_ref, in_ref, mlp_ref)
    stage_ref[...] = live_cells(facts_ref, anchor_ref, EDGE_COUNTS, result)
    second = pltpu.make_async_copy(stage_ref, result_ref.at[:, block], sems.at[1])
    second.start()
    first.wait()
    second.wait()


def call(body, outs, scalars, arrays, flops, scratch=(), spaces=None, out_spaces=None):
    spaces = spaces or [pltpu.VMEM] * len(arrays)
    out = [pl.BlockSpec(memory_space=space) for space in out_spaces or [pltpu.VMEM] * len(outs)]
    moved = sum(math.prod(a.shape) * a.dtype.itemsize for a in arrays)
    single = len(outs) == 1
    arrays = [
        pltpu.with_memory_space_constraint(array, space) if space == pltpu.HBM else array
        for array, space in zip(arrays, spaces)
    ]
    return pl.pallas_call(
        body,
        out_shape=outs[0] if single else outs,
        in_specs=[pl.BlockSpec(memory_space=pltpu.SMEM)] * len(scalars)
        + [pl.BlockSpec(memory_space=space) for space in spaces],
        out_specs=out[0] if single else out,
        scratch_shapes=scratch,
        compiler_params=pltpu.CompilerParams(vmem_limit_bytes=24 * 1024 * 1024),
        cost_estimate=pl.CostEstimate(flops=flops, bytes_accessed=moved, transcendentals=0),
    )(*scalars, *arrays)


def local(
    fields,
    counts,
    shifts,
    norm_gains,
    window_qkv,
    window_out,
    column_qkv,
    column_out,
    mlp_in,
    mlp_out,
):
    levels, row_count, cells, width = fields.shape
    blocks = row_count // WIN_ROWS
    tokens = WIN_ROWS * cells
    total = levels * tokens
    runs = levels * WIN_ROWS
    tiles = lax.axis_size("lon")
    circle = cells * tiles
    anchor = jnp.full((8, LANES), lax.axis_index("lon") * cells, jnp.int32)

    weights = [norm_gains, window_qkv, window_out]
    sent, edge, other, facts, *weights = call(
        pack_kernel,
        [
            jax.ShapeDtypeStruct((1 + runs, cells, width), BF16),
            jax.ShapeDtypeStruct((runs, cells, width), BF16),
            jax.ShapeDtypeStruct((runs, cells, width), BF16),
            jax.ShapeDtypeStruct((FACTS, LANES), jnp.int32),
        ]
        + [jax.ShapeDtypeStruct(array.shape, array.dtype) for array in weights],
        [],
        [shifts, counts, fields.reshape(levels, blocks, WIN_ROWS, cells, width)] + weights,
        10**6,
        [
            pltpu.SMEM(shifts.shape, jnp.int32),
            pltpu.SMEM(counts.shape, jnp.int32),
            pltpu.VMEM((levels, blocks, WIN_ROWS, cells, width), BF16),
            pltpu.SemaphoreType.DMA((6,)),
        ],
        [pltpu.HBM] * 6,
    )
    west = [(tile, (tile - 1) % tiles) for tile in range(tiles)]
    behind = lax.ppermute(sent, "lon", [pair[::-1] for pair in west])
    ahead_other = lax.ppermute(other, "lon", west)

    one = jax.ShapeDtypeStruct((total, width), BF16)
    three = jax.ShapeDtypeStruct((3, total, width), BF16)
    done_edge, done_other = call(own_kernel, [three, three], [], [edge, other] + weights[:2], 10**9)
    ahead_edge = lax.ppermute(edge, "lon", west)
    resident_other, normed_other = call(
        functools.partial(window_both_kernel, circle),
        [one, one],
        [],
        [facts, anchor, other, done_other, behind, ahead_other] + weights,
        10**9,
    )
    resident_edge, normed_edge = call(
        functools.partial(window_edge_kernel, circle),
        [one, one],
        [],
        [facts, anchor, edge, done_edge, behind, ahead_edge] + weights + [resident_other],
        10**9,
        spaces=[pltpu.VMEM] * (6 + len(weights)) + [pl.ANY],
    )

    groups = [[first, first + 1] for first in range(0, 2 * CORES, CORES)]
    swap = [(n, n ^ CORES) for n in range(2 * CORES)]

    def gather(part, other):
        return lax.all_gather(jnp.stack([part, other]), "lev", tiled=True, axis_index_groups=groups)

    swapped_other, swapped_edge = [lax.ppermute(part, "lev", swap) for part in (normed_other, normed_edge)]
    weights = [norm_gains, column_qkv, column_out, mlp_in, mlp_out]
    first = call(
        column_first_kernel,
        [jax.ShapeDtypeStruct((levels, tokens, width), BF16)],
        [],
        [facts, anchor, resident_other, normed_other, gather(normed_other, swapped_other)] + weights,
        10**9,
    )
    first, swapped_edge = lax.optimization_barrier((first, swapped_edge))
    result = call(
        column_last_kernel,
        [jax.ShapeDtypeStruct((levels, blocks, tokens, width), BF16)],
        [],
        [shifts, facts, anchor, resident_edge, normed_edge, gather(normed_edge, swapped_edge), first] + weights,
        10**9,
        [
            pltpu.VMEM((levels, tokens, width), BF16),
            pltpu.SMEM(shifts.shape, jnp.int32),
            pltpu.SemaphoreType.DMA((3,)),
        ],
        [pltpu.HBM] + [pltpu.VMEM] * (6 + len(weights)),
        out_spaces=[pltpu.HBM],
    )
    return result.reshape(fields.shape)


def solution(mesh):
    return jax.shard_map(
        local,
        mesh=mesh,
        in_specs=(P("lev", None, "lon", None), P(), P(), P(), P(), P(), P(), P(), P(), P()),
        out_specs=P("lev", None, "lon", None),
        check_vma=False,
    )
```

```python
import functools
import math

import jax
import jax.numpy as jnp
from jax import lax
from jax.experimental import pallas as pl
from jax.experimental.pallas import tpu as pltpu
from jax.sharding import PartitionSpec as P

HEADS = 12
WIN_ROWS = 4
WIN_LON = 16
EPSILON = 1e-05
LANES = 128
CORES = 2
F32 = jnp.float32
BF16 = jnp.bfloat16


def layer_norm(values, gain_row):
    average = jnp.mean(values, axis=-1, keepdims=True)
    centred = values - average
    variance = jnp.mean(centred * centred, axis=-1, keepdims=True)
    return (centred * lax.rsqrt(variance + EPSILON) * gain_row).astype(BF16)


def dot32(left, right):
    return jnp.dot(left, right, preferred_element_type=F32)


def attend(units, allowed, head_size):
    count, width = units[0][0].shape
    per = LANES // head_size
    scale = math.log2(math.e) / math.sqrt(head_size)
    head_of_lane = lax.broadcasted_iota(jnp.int32, (count, LANES), 1) // head_size
    both = jnp.concatenate([head_of_lane, head_of_lane], axis=1)
    ones = jnp.ones((units[0][1].shape[0], LANES), BF16)
    groups = width // LANES
    cuts = [slice(group * LANES, (group + 1) * LANES) for group in range(groups)]
    jobs = [[part[:, at] for part in unit] for unit in units for at in cuts]
    scores = []
    for queries, keys, _ in jobs:
        spread = jnp.concatenate(
            [jnp.where(head_of_lane == head, queries, jnp.zeros_like(queries)) for head in range(per)], axis=0
        )
        scores.append(
            lax.dot_general(spread, keys, (((1,), (1,)), ((), ())), preferred_element_type=F32)
        )
    weights = []
    for score in scores:
        score = jnp.where(allowed[None], score.reshape(per, count, -1), -jnp.inf)
        highest = jnp.max(score, axis=-1, keepdims=True)
        weights.append(jnp.exp2((score - highest) * scale).astype(BF16).reshape(per * count, -1))
    mixes = [
        dot32(weight, jnp.concatenate([values, ones], axis=1)).reshape(per, count, 2 * LANES)
        for weight, (_, _, values) in zip(weights, jobs)
    ]
    pieces = []
    for mixed in mixes:
        picked = mixed[0]
        for head in range(1, per):
            picked = jnp.where(both == head, mixed[head], picked)
        pieces.append((picked[:, :LANES] / picked[:, LANES:]).astype(BF16))
    return [
        jnp.concatenate(pieces[first : first + groups], axis=1) for first in range(0, len(pieces), groups)
    ]


SHIFT, BOTH_COUNTS, EDGE_COUNTS, FACTS = 0, 1, 5, 16


def fact(facts_ref, row):
    return facts_ref[row : row + 1, :1]


def count_of_row(facts_ref, first, rows):
    wanted = fact(facts_ref, first)
    for row in range(1, WIN_ROWS):
        wanted = jnp.where(rows == row, fact(facts_ref, first + row), wanted)
    return wanted


def edge_block(shifts_ref):
    return jnp.where(shifts_ref[0] == WIN_LON - 1, 0, 1)


def pack_kernel(
    shifts_hbm, counts_hbm, fields_hbm, east_ref, edge_ref, other_ref, facts_ref, shifts_ref, counts_ref, fields_ref,
    sems,
):
    runs, cells, width = edge_ref.shape
    moves = [(shifts_hbm, shifts_ref), (counts_hbm, counts_ref), (fields_hbm, fields_ref)]
    copies = [pltpu.make_async_copy(*ends, sems.at[n]) for n, ends in enumerate(moves)]
    for copy in copies:
        copy.start()
    for copy in copies:
        copy.wait()
    block = edge_block(shifts_ref)
    edge = fields_ref[:, block].reshape(runs, cells, width)
    other = fields_ref[:, 1 - block].reshape(runs, cells, width)
    edge_ref[...] = edge
    other_ref[...] = east_ref[1:] = other
    edge = edge.astype(F32)
    east_ref[0] = jnp.concatenate([edge[run, cells - 1 :] for run in range(runs)], axis=0).astype(BF16)
    numbers = [shifts_ref[1 - block]]
    numbers += [counts_ref[(1 - block) * WIN_ROWS + row] for row in range(WIN_ROWS)]
    numbers += [counts_ref[block * WIN_ROWS + row] for row in range(WIN_ROWS)]
    place = lax.broadcasted_iota(jnp.int32, facts_ref.shape, 0)
    facts = jnp.zeros(facts_ref.shape, jnp.int32)
    for row, number in enumerate(numbers):
        facts = jnp.where(place == row, number, facts)
    facts_ref[...] = facts


def own_kernel(edge_ref, other_ref, gains_ref, qkv_ref, edge_out_ref, other_out_ref):
    total, width = edge_out_ref.shape[1:]
    outs = (edge_out_ref, other_out_ref)
    normed = [
        layer_norm(own[...].reshape(total, width).astype(F32), gains_ref[0:1]) for own in (edge_ref, other_ref)
    ]
    for n in range(3):
        for part, out_ref in zip(normed, outs):
            out_ref[n] = dot32(part, qkv_ref[n]).astype(BF16)


def window_block(
    circle, shift, counts_row, other, own, done_ref, facts_ref, anchor_ref, gains_ref, qkv_ref, out_w_ref, result_ref,
    normed_ref,
):
    total, width = own.shape
    tokens = WIN_ROWS * WIN_LON
    anchor = anchor_ref[:1, :1]
    normed = layer_norm(other, gains_ref[0:1])
    keys, values = [dot32(normed, qkv_ref[n]).astype(BF16) for n in (1, 2)]

    shape = (tokens, 2 * tokens)
    query_place = lax.broadcasted_iota(jnp.int32, shape, 0) % WIN_LON
    key = lax.broadcasted_iota(jnp.int32, shape, 1)
    where = key % WIN_LON
    here = key < tokens
    cell = anchor + where
    away = jnp.where(where < shift, cell + WIN_LON, cell - WIN_LON + circle)
    cell = jnp.where(here, cell, jnp.where(away >= circle, away - circle, away))
    same = (query_place < shift) == (where < shift)
    allowed = (here == same) & (cell < count_of_row(facts_ref, counts_row, (key // WIN_LON) % WIN_ROWS))
    units = []
    for first in range(0, total, tokens):
        at = slice(first, first + tokens)
        units.append(
            (
                done_ref[0, at],
                jnp.concatenate([done_ref[1, at], keys[at]], axis=0),
                jnp.concatenate([done_ref[2, at], values[at]], axis=0),
            )
        )
    mixed = attend(units, allowed, width // HEADS)
    resident = (own + dot32(jnp.concatenate(mixed, axis=0), out_w_ref[...])).astype(BF16)
    result_ref[...] = resident
    normed_ref[...] = layer_norm(resident.astype(F32), gains_ref[1:2])


def window_edge_kernel(
    circle, facts_ref, anchor_ref, own_ref, done_ref, behind_ref, ahead_ref, gains_ref, qkv_ref, out_w_ref, _,
    result_ref, normed_ref,
):
    total, width = result_ref.shape
    cells = behind_ref[0].astype(F32)
    behind = jnp.concatenate(
        [jnp.broadcast_to(cells[n : n + 1], (WIN_LON, width)) for n in range(total // WIN_LON)], axis=0
    )
    place = lax.broadcasted_iota(jnp.int32, (total, width), 0) % WIN_LON
    other = jnp.where(place == WIN_LON - 1, behind, ahead_ref[...].reshape(total, width).astype(F32))
    window_block(
        circle, WIN_LON - 1, EDGE_COUNTS, other, own_ref[...].reshape(total, width).astype(F32), done_ref, facts_ref,
        anchor_ref, gains_ref, qkv_ref, out_w_ref, result_ref, normed_ref,
    )


def window_both_kernel(
    circle, facts_ref, anchor_ref, own_ref, done_ref, behind_ref, ahead_ref, gains_ref, qkv_ref, out_w_ref, result_ref,
    normed_ref,
):
    total, width = result_ref.shape
    shift = fact(facts_ref, SHIFT)
    place = lax.broadcasted_iota(jnp.int32, (total, width), 0) % WIN_LON
    behind = behind_ref[1:].reshape(total, width).astype(F32)
    ahead = ahead_ref[...].reshape(total, width).astype(F32)
    window_block(
        circle, shift, BOTH_COUNTS, jnp.where(place < shift, ahead, behind),
        own_ref[...].reshape(total, width).astype(F32), done_ref, facts_ref, anchor_ref, gains_ref, qkv_ref, out_w_ref,
        result_ref, normed_ref,
    )


def column_attend(normed_ref, gathered_ref, qkv_ref):
    parts, tokens, width = gathered_ref.shape
    total = parts * tokens
    normed = gathered_ref[...].reshape(total, width)
    queries = dot32(normed_ref[...], qkv_ref[0]).astype(BF16)
    keys, values = [dot32(normed, qkv_ref[n]).astype(BF16) for n in (1, 2)]

    span = WIN_ROWS * WIN_LON
    levels = tokens // span
    all_levels = total // span
    queries = queries.reshape(levels, WIN_ROWS, WIN_LON, width)
    keys = keys.reshape(all_levels, WIN_ROWS, WIN_LON, width)
    values = values.reshape(all_levels, WIN_ROWS, WIN_LON, width)
    shape = (levels * WIN_LON, all_levels * WIN_LON)
    allowed = (
        lax.broadcasted_iota(jnp.int32, shape, 0) % WIN_LON
        == lax.broadcasted_iota(jnp.int32, shape, 1) % WIN_LON
    )
    mixed = []
    for first in range(0, WIN_ROWS, 2):
        units = [
            (
                queries[:, row].reshape(levels * WIN_LON, width),
                keys[:, row].reshape(all_levels * WIN_LON, width),
                values[:, row].reshape(all_levels * WIN_LON, width),
            )
            for row in (first, first + 1)
        ]
        mixed += attend(units, allowed, width // HEADS)
    mixed = jnp.concatenate([part.reshape(levels, 1, WIN_LON, width) for part in mixed], axis=1)
    return mixed.reshape(tokens, width)


def feed_forward(mixed, resident_ref, gains_ref, out_w_ref, in_ref, mlp_ref):
    tokens = mixed.shape[0]
    half = tokens // 2
    halves = [slice(0, half), slice(half, tokens)]
    updated = [
        (resident_ref[at].astype(F32) + dot32(mixed[at], out_w_ref[...])).astype(BF16) for at in halves
    ]
    normed = [layer_norm(part.astype(F32), gains_ref[2:3]) for part in updated]
    inner = [dot32(part, in_ref[...]) for part in normed]
    inner = [jax.nn.gelu(part).astype(BF16) for part in inner]
    result = [part.astype(F32) + dot32(act, mlp_ref[...]) for part, act in zip(updated, inner)]
    return jnp.concatenate(result, axis=0)


def live_cells(facts_ref, anchor_ref, counts_row, values):
    tokens = WIN_ROWS * WIN_LON
    width = values.shape[1]
    token = lax.broadcasted_iota(jnp.int32, (tokens, width), 0)
    live = anchor_ref[:1, :1] + token % WIN_LON < count_of_row(facts_ref, counts_row, token // WIN_LON)
    return jnp.where(live[None], values.reshape(-1, tokens, width), 0.0).astype(BF16)


def column_first_kernel(
    facts_ref, anchor_ref, resident_ref, normed_ref, gathered_ref, gains_ref, qkv_ref, out_w_ref, in_ref, mlp_ref,
    result_ref,
):
    mixed = column_attend(normed_ref, gathered_ref, qkv_ref)
    result = feed_forward(mixed, resident_ref, gains_ref, out_w_ref, in_ref, mlp_ref)
    result_ref[...] = live_cells(facts_ref, anchor_ref, BOTH_COUNTS, result)


def column_last_kernel(
    shifts_hbm, facts_ref, anchor_ref, resident_ref, normed_ref, gathered_ref, first_ref, gains_ref, qkv_ref,
    out_w_ref, in_ref, mlp_ref, result_ref, stage_ref, shifts_ref, sems,
):
    shifts_copy = pltpu.make_async_copy(shifts_hbm, shifts_ref, sems.at[2])
    shifts_copy.start()
    mixed = column_attend(normed_ref, gathered_ref, qkv_ref)
    shifts_copy.wait()
    block = edge_block(shifts_ref)
    first = pltpu.make_async_copy(first_ref, result_ref.at[:, 1 - block], sems.at[0])
    first.start()
    result = feed_forward(mixed, resident_ref, gains_ref, out_w_ref, in_ref, mlp_ref)
    stage_ref[...] = live_cells(facts_ref, anchor_ref, EDGE_COUNTS, result)
    second = pltpu.make_async_copy(stage_ref, result_ref.at[:, block], sems.at[1])
    second.start()
    first.wait()
    second.wait()


def call(body, outs, scalars, arrays, flops, scratch=(), spaces=None, out_spaces=None):
    spaces = spaces or [pltpu.VMEM] * len(arrays)
    out = [pl.BlockSpec(memory_space=space) for space in out_spaces or [pltpu.VMEM] * len(outs)]
    moved = sum(math.prod(a.shape) * a.dtype.itemsize for a in arrays)
    single = len(outs) == 1
    arrays = [
        pltpu.with_memory_space_constraint(array, space) if space == pltpu.HBM else array
        for array, space in zip(arrays, spaces)
    ]
    return pl.pallas_call(
        body,
        out_shape=outs[0] if single else outs,
        in_specs=[pl.BlockSpec(memory_space=pltpu.SMEM)] * len(scalars)
        + [pl.BlockSpec(memory_space=space) for space in spaces],
        out_specs=out[0] if single else out,
        scratch_shapes=scratch,
        compiler_params=pltpu.CompilerParams(vmem_limit_bytes=24 * 1024 * 1024),
        cost_estimate=pl.CostEstimate(flops=flops, bytes_accessed=moved, transcendentals=0),
    )(*scalars, *arrays)


def local(
    fields,
    counts,
    shifts,
    norm_gains,
    window_qkv,
    window_out,
    column_qkv,
    column_out,
    mlp_in,
    mlp_out,
):
    levels, row_count, cells, width = fields.shape
    blocks = row_count // WIN_ROWS
    tokens = WIN_ROWS * cells
    total = levels * tokens
    runs = levels * WIN_ROWS
    tiles = lax.axis_size("lon")
    circle = cells * tiles
    anchor = jnp.full((8, LANES), lax.axis_index("lon") * cells, jnp.int32)

    weights = [norm_gains, window_qkv, window_out]
    sent, edge, other, facts = call(
        pack_kernel,
        [
            jax.ShapeDtypeStruct((1 + runs, cells, width), BF16),
            jax.ShapeDtypeStruct((runs, cells, width), BF16),
            jax.ShapeDtypeStruct((runs, cells, width), BF16),
            jax.ShapeDtypeStruct((FACTS, LANES), jnp.int32),
        ],
        [],
        [shifts, counts, fields.reshape(levels, blocks, WIN_ROWS, cells, width)],
        10**10,
        [
            pltpu.SMEM(shifts.shape, jnp.int32),
            pltpu.SMEM(counts.shape, jnp.int32),
            pltpu.VMEM((levels, blocks, WIN_ROWS, cells, width), BF16),
            pltpu.SemaphoreType.DMA((6,)),
        ],
        [pltpu.HBM] * 3,
    )
    west = [(tile, (tile - 1) % tiles) for tile in range(tiles)]
    behind = lax.ppermute(sent, "lon", [pair[::-1] for pair in west])
    ahead_other = lax.ppermute(other, "lon", west)

    one = jax.ShapeDtypeStruct((total, width), BF16)
    three = jax.ShapeDtypeStruct((3, total, width), BF16)
    done_edge, done_other = call(own_kernel, [three, three], [], [edge, other] + weights[:2], 10**9)
    ahead_edge = lax.ppermute(edge, "lon", west)
    resident_other, normed_other = call(
        functools.partial(window_both_kernel, circle),
        [one, one],
        [],
        [facts, anchor, other, done_other, behind, ahead_other] + weights,
        10**9,
    )
    resident_edge, normed_edge = call(
        functools.partial(window_edge_kernel, circle),
        [one, one],
        [],
        [facts, anchor, edge, done_edge, behind, ahead_edge] + weights + [resident_other],
        10**9,
        spaces=[pltpu.VMEM] * (6 + len(weights)) + [pl.ANY],
    )

    groups = [[first, first + 1] for first in range(0, 2 * CORES, CORES)]
    swap = [(n, n ^ CORES) for n in range(2 * CORES)]

    def gather(part, other):
        return lax.all_gather(jnp.stack([part, other]), "lev", tiled=True, axis_index_groups=groups)

    swapped_other, swapped_edge = [lax.ppermute(part, "lev", swap) for part in (normed_other, normed_edge)]
    weights = [norm_gains, column_qkv, column_out, mlp_in, mlp_out]
    first = call(
        column_first_kernel,
        [jax.ShapeDtypeStruct((levels, tokens, width), BF16)],
        [],
        [facts, anchor, resident_other, normed_other, gather(normed_other, swapped_other)] + weights,
        10**9,
    )
    first, swapped_edge = lax.optimization_barrier((first, swapped_edge))
    result = call(
        column_last_kernel,
        [jax.ShapeDtypeStruct((levels, blocks, tokens, width), BF16)],
        [],
        [shifts, facts, anchor, resident_edge, normed_edge, gather(normed_edge, swapped_edge), first] + weights,
        10**9,
        [
            pltpu.VMEM((levels, tokens, width), BF16),
            pltpu.SMEM(shifts.shape, jnp.int32),
            pltpu.SemaphoreType.DMA((3,)),
        ],
        [pltpu.HBM] + [pltpu.VMEM] * (6 + len(weights)),
        out_spaces=[pltpu.HBM],
    )
    return result.reshape(fields.shape)


def solution(mesh):
    return jax.shard_map(
        local,
        mesh=mesh,
        in_specs=(P("lev", None, "lon", None), P(), P(), P(), P(), P(), P(), P(), P(), P()),
        out_specs=P("lev", None, "lon", None),
        check_vma=False,
    )
```

```python
import functools
import math

import jax
import jax.numpy as jnp
from jax import lax
from jax.experimental import pallas as pl
from jax.experimental.pallas import tpu as pltpu
from jax.sharding import PartitionSpec as P

HEADS = 12
WIN_ROWS = 4
WIN_LON = 16
EPSILON = 1e-05
LANES = 128
CORES = 2
F32 = jnp.float32
BF16 = jnp.bfloat16


def layer_norm(values, gain_row):
    average = jnp.mean(values, axis=-1, keepdims=True)
    centred = values - average
    variance = jnp.mean(centred * centred, axis=-1, keepdims=True)
    return (centred * lax.rsqrt(variance + EPSILON) * gain_row).astype(BF16)


def dot32(left, right):
    return jnp.dot(left, right, preferred_element_type=F32)


def project_queries(normed, weights):
    scale = math.log2(math.e) / math.sqrt(weights.shape[1] // HEADS)
    return (dot32(normed, weights) * scale).astype(BF16)


def attend(units, allowed, head_size, exp_type):
    count, width = units[0][0].shape
    per = LANES // head_size
    head_of_lane = lax.broadcasted_iota(jnp.int32, (count, LANES), 1) // head_size
    both = jnp.concatenate([head_of_lane, head_of_lane], axis=1)
    ones = jnp.ones((units[0][1].shape[0], LANES), BF16)
    groups = width // LANES
    cuts = [slice(group * LANES, (group + 1) * LANES) for group in range(groups)]
    jobs = [[part[:, at] for part in unit] for unit in units for at in cuts]
    scores = []
    for queries, keys, _ in jobs:
        spread = jnp.concatenate(
            [jnp.where(head_of_lane == head, queries, jnp.zeros_like(queries)) for head in range(per)], axis=0
        )
        scores.append(
            lax.dot_general(spread, keys, (((1,), (1,)), ((), ())), preferred_element_type=F32)
        )
    weights = []
    for score in scores:
        score = jnp.where(allowed[None], score.reshape(per, count, -1), -jnp.inf)
        highest = jnp.max(score, axis=-1, keepdims=True)
        weights.append(jnp.exp2((score - highest).astype(exp_type)).astype(BF16).reshape(per * count, -1))
    mixes = [
        dot32(weight, jnp.concatenate([values, ones], axis=1)).reshape(per, count, 2 * LANES)
        for weight, (_, _, values) in zip(weights, jobs)
    ]
    pieces = []
    for mixed in mixes:
        picked = mixed[0]
        for head in range(1, per):
            picked = jnp.where(both == head, mixed[head], picked)
        pieces.append((picked[:, :LANES] / picked[:, LANES:]).astype(BF16))
    return [
        jnp.concatenate(pieces[first : first + groups], axis=1) for first in range(0, len(pieces), groups)
    ]


SHIFT, BOTH_COUNTS, EDGE_COUNTS, FACTS = 0, 1, 5, 16


def fact(facts_ref, row):
    return facts_ref[row : row + 1, :1]


def count_of_row(facts_ref, first, rows):
    wanted = fact(facts_ref, first)
    for row in range(1, WIN_ROWS):
        wanted = jnp.where(rows == row, fact(facts_ref, first + row), wanted)
    return wanted


def edge_block(shifts_ref):
    return jnp.where(shifts_ref[0] == WIN_LON - 1, 0, 1)


def pack_kernel(
    shifts_hbm, counts_hbm, fields_hbm, east_ref, edge_ref, other_ref, facts_ref, shifts_ref, counts_ref, fields_ref,
    sems,
):
    runs, cells, width = edge_ref.shape
    moves = [(shifts_hbm, shifts_ref), (counts_hbm, counts_ref), (fields_hbm, fields_ref)]
    copies = [pltpu.make_async_copy(*ends, sems.at[n]) for n, ends in enumerate(moves)]
    for copy in copies:
        copy.start()
    for copy in copies:
        copy.wait()
    block = edge_block(shifts_ref)
    edge = fields_ref[:, block].reshape(runs, cells, width)
    other = fields_ref[:, 1 - block].reshape(runs, cells, width)
    edge_ref[...] = edge
    other_ref[...] = east_ref[1:] = other
    edge = edge.astype(F32)
    east_ref[0] = jnp.concatenate([edge[run, cells - 1 :] for run in range(runs)], axis=0).astype(BF16)
    numbers = [shifts_ref[1 - block]]
    numbers += [counts_ref[(1 - block) * WIN_ROWS + row] for row in range(WIN_ROWS)]
    numbers += [counts_ref[block * WIN_ROWS + row] for row in range(WIN_ROWS)]
    place = lax.broadcasted_iota(jnp.int32, facts_ref.shape, 0)
    facts = jnp.zeros(facts_ref.shape, jnp.int32)
    for row, number in enumerate(numbers):
        facts = jnp.where(place == row, number, facts)
    facts_ref[...] = facts


def own_kernel(edge_ref, other_ref, gains_ref, qkv_ref, edge_out_ref, other_out_ref):
    total, width = edge_out_ref.shape[1:]
    outs = (edge_out_ref, other_out_ref)
    normed = [
        layer_norm(own[...].reshape(total, width).astype(F32), gains_ref[0:1]) for own in (edge_ref, other_ref)
    ]
    for n in range(3):
        for part, out_ref in zip(normed, outs):
            project = dot32 if n > 0 else project_queries
            out_ref[n] = project(part, qkv_ref[n]).astype(BF16)


def window_block(
    circle, shift, counts_row, other, own, done_ref, facts_ref, anchor_ref, gains_ref, qkv_ref, out_w_ref, result_ref,
    normed_ref,
):
    total, width = own.shape
    tokens = WIN_ROWS * WIN_LON
    anchor = anchor_ref[:1, :1]
    normed = layer_norm(other, gains_ref[0:1])
    keys, values = [dot32(normed, qkv_ref[n]).astype(BF16) for n in (1, 2)]

    shape = (tokens, 2 * tokens)
    query_place = lax.broadcasted_iota(jnp.int32, shape, 0) % WIN_LON
    key = lax.broadcasted_iota(jnp.int32, shape, 1)
    where = key % WIN_LON
    here = key < tokens
    cell = anchor + where
    away = jnp.where(where < shift, cell + WIN_LON, cell - WIN_LON + circle)
    cell = jnp.where(here, cell, jnp.where(away >= circle, away - circle, away))
    same = (query_place < shift) == (where < shift)
    allowed = (here == same) & (cell < count_of_row(facts_ref, counts_row, (key // WIN_LON) % WIN_ROWS))
    units = []
    for first in range(0, total, tokens):
        at = slice(first, first + tokens)
        units.append(
            (
                done_ref[0, at],
                jnp.concatenate([done_ref[1, at], keys[at]], axis=0),
                jnp.concatenate([done_ref[2, at], values[at]], axis=0),
            )
        )
    mixed = attend(units, allowed, width // HEADS, F32)
    resident = (own + dot32(jnp.concatenate(mixed, axis=0), out_w_ref[...])).astype(BF16)
    result_ref[...] = resident
    normed_ref[...] = layer_norm(resident.astype(F32), gains_ref[1:2])


def window_edge_kernel(
    circle, facts_ref, anchor_ref, own_ref, done_ref, behind_ref, ahead_ref, gains_ref, qkv_ref, out_w_ref, _,
    result_ref, normed_ref,
):
    total, width = result_ref.shape
    cells = behind_ref[0].astype(F32)
    behind = jnp.concatenate(
        [jnp.broadcast_to(cells[n : n + 1], (WIN_LON, width)) for n in range(total // WIN_LON)], axis=0
    )
    place = lax.broadcasted_iota(jnp.int32, (total, width), 0) % WIN_LON
    other = jnp.where(place == WIN_LON - 1, behind, ahead_ref[...].reshape(total, width).astype(F32))
    window_block(
        circle, WIN_LON - 1, EDGE_COUNTS, other, own_ref[...].reshape(total, width).astype(F32), done_ref, facts_ref,
        anchor_ref, gains_ref, qkv_ref, out_w_ref, result_ref, normed_ref,
    )


def window_both_kernel(
    circle, facts_ref, anchor_ref, own_ref, done_ref, behind_ref, ahead_ref, gains_ref, qkv_ref, out_w_ref, result_ref,
    normed_ref,
):
    total, width = result_ref.shape
    shift = fact(facts_ref, SHIFT)
    place = lax.broadcasted_iota(jnp.int32, (total, width), 0) % WIN_LON
    behind = behind_ref[1:].reshape(total, width).astype(F32)
    ahead = ahead_ref[...].reshape(total, width).astype(F32)
    window_block(
        circle, shift, BOTH_COUNTS, jnp.where(place < shift, ahead, behind),
        own_ref[...].reshape(total, width).astype(F32), done_ref, facts_ref, anchor_ref, gains_ref, qkv_ref, out_w_ref,
        result_ref, normed_ref,
    )


def column_attend(queries, keys, values):
    tokens, width = queries.shape
    total = keys.shape[0]
    span = WIN_ROWS * WIN_LON
    levels = tokens // span
    all_levels = total // span
    queries = queries.reshape(levels, WIN_ROWS, WIN_LON, width)
    keys = keys.reshape(all_levels, WIN_ROWS, WIN_LON, width)
    values = values.reshape(all_levels, WIN_ROWS, WIN_LON, width)
    shape = (levels * WIN_LON, all_levels * WIN_LON)
    allowed = (
        lax.broadcasted_iota(jnp.int32, shape, 0) % WIN_LON
        == lax.broadcasted_iota(jnp.int32, shape, 1) % WIN_LON
    )
    mixed = []
    for first in range(0, WIN_ROWS, 2):
        units = [
            (
                queries[:, row].reshape(levels * WIN_LON, width),
                keys[:, row].reshape(all_levels * WIN_LON, width),
                values[:, row].reshape(all_levels * WIN_LON, width),
            )
            for row in (first, first + 1)
        ]
        mixed += attend(units, allowed, width // HEADS, BF16)
    mixed = jnp.concatenate([part.reshape(levels, 1, WIN_LON, width) for part in mixed], axis=1)
    return mixed.reshape(tokens, width)


def feed_forward(mixed, resident_ref, gains_ref, out_w_ref, in_ref, mlp_ref):
    tokens = mixed.shape[0]
    half = tokens // 2
    halves = [slice(0, half), slice(half, tokens)]
    updated = [
        (resident_ref[at].astype(F32) + dot32(mixed[at], out_w_ref[...])).astype(BF16) for at in halves
    ]
    normed = [layer_norm(part.astype(F32), gains_ref[2:3]) for part in updated]
    inner = [dot32(part, in_ref[...]) for part in normed]
    inner = [jax.nn.gelu(part).astype(BF16) for part in inner]
    result = [part.astype(F32) + dot32(act, mlp_ref[...]) for part, act in zip(updated, inner)]
    return jnp.concatenate(result, axis=0)


def live_cells(facts_ref, anchor_ref, counts_row, values):
    tokens = WIN_ROWS * WIN_LON
    width = values.shape[1]
    token = lax.broadcasted_iota(jnp.int32, (tokens, width), 0)
    live = anchor_ref[:1, :1] + token % WIN_LON < count_of_row(facts_ref, counts_row, token // WIN_LON)
    return jnp.where(live[None], values.reshape(-1, tokens, width), 0.0).astype(BF16)


def column_first_kernel(
    facts_ref, anchor_ref, resident_ref, normed_ref, gathered_ref, gains_ref, qkv_ref, out_w_ref, in_ref, mlp_ref,
    result_ref,
):
    queries = project_queries(normed_ref[...], qkv_ref[0])
    gathered = gathered_ref[...].reshape(-1, resident_ref.shape[1])
    keys, values = [dot32(gathered, qkv_ref[n]).astype(BF16) for n in (1, 2)]
    mixed = column_attend(queries, keys, values)
    result = feed_forward(mixed, resident_ref, gains_ref, out_w_ref, in_ref, mlp_ref)
    result_ref[...] = live_cells(facts_ref, anchor_ref, BOTH_COUNTS, result)


def column_own_kernel(normed_ref, qkv_ref, _, result_ref):
    normed = normed_ref[...]
    result_ref[0] = project_queries(normed, qkv_ref[0])
    for n in (1, 2):
        result_ref[n] = dot32(normed, qkv_ref[n]).astype(BF16)


def column_last_kernel(
    core_ref, shifts_hbm, facts_ref, anchor_ref, resident_ref, done_ref, swapped_ref, gathered_ref, first_ref,
    gains_ref, qkv_ref, out_w_ref, in_ref, mlp_ref, result_ref, stage_ref, shifts_ref, sems,
):
    shifts_copy = pltpu.make_async_copy(shifts_hbm, shifts_ref, sems.at[2])
    shifts_copy.start()
    parts, tokens, width = gathered_ref.shape
    half = parts // CORES
    partner = gathered_ref[pl.ds((1 - core_ref[0]) * half, half)].reshape(half * tokens, width)
    rest = jnp.concatenate([swapped_ref[...], partner], axis=0)
    keys, values = [
        jnp.concatenate([done_ref[n], dot32(rest, qkv_ref[n]).astype(BF16)], axis=0) for n in (1, 2)
    ]
    mixed = column_attend(done_ref[0], keys, values)
    shifts_copy.wait()
    block = edge_block(shifts_ref)
    first = pltpu.make_async_copy(first_ref, result_ref.at[:, 1 - block], sems.at[0])
    first.start()
    result = feed_forward(mixed, resident_ref, gains_ref, out_w_ref, in_ref, mlp_ref)
    stage_ref[...] = live_cells(facts_ref, anchor_ref, EDGE_COUNTS, result)
    second = pltpu.make_async_copy(stage_ref, result_ref.at[:, block], sems.at[1])
    second.start()
    first.wait()
    second.wait()


def call(body, outs, scalars, arrays, flops, scratch=(), spaces=None, out_spaces=None):
    spaces = spaces or [pltpu.VMEM] * len(arrays)
    out = [pl.BlockSpec(memory_space=space) for space in out_spaces or [pltpu.VMEM] * len(outs)]
    moved = sum(math.prod(a.shape) * a.dtype.itemsize for a in arrays)
    single = len(outs) == 1
    arrays = [
        pltpu.with_memory_space_constraint(array, space) if space == pltpu.HBM else array
        for array, space in zip(arrays, spaces)
    ]
    return pl.pallas_call(
        body,
        out_shape=outs[0] if single else outs,
        in_specs=[pl.BlockSpec(memory_space=pltpu.SMEM)] * len(scalars)
        + [pl.BlockSpec(memory_space=space) for space in spaces],
        out_specs=out[0] if single else out,
        scratch_shapes=scratch,
        compiler_params=pltpu.CompilerParams(vmem_limit_bytes=24 * 1024 * 1024),
        cost_estimate=pl.CostEstimate(flops=flops, bytes_accessed=moved, transcendentals=0),
    )(*scalars, *arrays)


def local(
    fields,
    counts,
    shifts,
    norm_gains,
    window_qkv,
    window_out,
    column_qkv,
    column_out,
    mlp_in,
    mlp_out,
):
    levels, row_count, cells, width = fields.shape
    blocks = row_count // WIN_ROWS
    tokens = WIN_ROWS * cells
    total = levels * tokens
    runs = levels * WIN_ROWS
    tiles = lax.axis_size("lon")
    circle = cells * tiles
    anchor = jnp.full((8, LANES), lax.axis_index("lon") * cells, jnp.int32)

    weights = [norm_gains, window_qkv, window_out]
    sent, edge, other, facts = call(
        pack_kernel,
        [
            jax.ShapeDtypeStruct((1 + runs, cells, width), BF16),
            jax.ShapeDtypeStruct((runs, cells, width), BF16),
            jax.ShapeDtypeStruct((runs, cells, width), BF16),
            jax.ShapeDtypeStruct((FACTS, LANES), jnp.int32),
        ],
        [],
        [shifts, counts, fields.reshape(levels, blocks, WIN_ROWS, cells, width)],
        10**10,
        [
            pltpu.SMEM(shifts.shape, jnp.int32),
            pltpu.SMEM(counts.shape, jnp.int32),
            pltpu.VMEM((levels, blocks, WIN_ROWS, cells, width), BF16),
            pltpu.SemaphoreType.DMA((6,)),
        ],
        [pltpu.HBM] * 3,
    )
    west = [(tile, (tile - 1) % tiles) for tile in range(tiles)]
    behind = lax.ppermute(sent, "lon", [pair[::-1] for pair in west])
    ahead_other = lax.ppermute(other, "lon", west)

    one = jax.ShapeDtypeStruct((total, width), BF16)
    three = jax.ShapeDtypeStruct((3, total, width), BF16)
    done_edge, done_other = call(own_kernel, [three, three], [], [edge, other] + weights[:2], 10**9)
    ahead_edge = lax.ppermute(edge, "lon", west)
    resident_other, normed_other = call(
        functools.partial(window_both_kernel, circle),
        [one, one],
        [],
        [facts, anchor, other, done_other, behind, ahead_other] + weights,
        10**9,
    )
    resident_edge, normed_edge = call(
        functools.partial(window_edge_kernel, circle),
        [one, one],
        [],
        [facts, anchor, edge, done_edge, behind, ahead_edge] + weights + [resident_other],
        10**9,
        spaces=[pltpu.VMEM] * (6 + len(weights)) + [pl.ANY],
    )

    groups = [[first, first + 1] for first in range(0, 2 * CORES, CORES)]
    swap = [(n, n ^ CORES) for n in range(2 * CORES)]

    def gather(part, other):
        return lax.all_gather(jnp.stack([part, other]), "lev", tiled=True, axis_index_groups=groups)

    swapped_other, swapped_edge = [lax.ppermute(part, "lev", swap) for part in (normed_other, normed_edge)]
    weights = [norm_gains, column_qkv, column_out, mlp_in, mlp_out]
    first = call(
        column_first_kernel,
        [jax.ShapeDtypeStruct((levels, tokens, width), BF16)],
        [],
        [facts, anchor, resident_other, normed_other, gather(normed_other, swapped_other)] + weights,
        10**9,
    )
    done = call(
        column_own_kernel,
        [three],
        [],
        [normed_edge, column_qkv, first],
        10**9,
        spaces=[pltpu.VMEM, pltpu.VMEM, pl.ANY],
    )
    first, swapped_edge = lax.optimization_barrier((first, swapped_edge))
    core = (lax.axis_index("lev") % CORES).astype(jnp.int32).reshape(1)
    result = call(
        column_last_kernel,
        [jax.ShapeDtypeStruct((levels, blocks, tokens, width), BF16)],
        [core],
        [shifts, facts, anchor, resident_edge, done, swapped_edge, gather(normed_edge, swapped_edge), first] + weights,
        10**9,
        [
            pltpu.VMEM((levels, tokens, width), BF16),
            pltpu.SMEM(shifts.shape, jnp.int32),
            pltpu.SemaphoreType.DMA((3,)),
        ],
        [pltpu.HBM] + [pltpu.VMEM] * (7 + len(weights)),
        out_spaces=[pltpu.HBM],
    )
    return result.reshape(fields.shape)


def solution(mesh):
    return jax.shard_map(
        local,
        mesh=mesh,
        in_specs=(P("lev", None, "lon", None), P(), P(), P(), P(), P(), P(), P(), P(), P()),
        out_specs=P("lev", None, "lon", None),
        check_vma=False,
    )
```

```python
import functools
import math

import jax
import jax.numpy as jnp
from jax import lax
from jax.experimental import pallas as pl
from jax.experimental.pallas import tpu as pltpu
from jax.sharding import PartitionSpec as P

HEADS = 12
WIN_ROWS = 4
WIN_LON = 16
EPSILON = 1e-05
LANES = 128
CORES = 2
F32 = jnp.float32
BF16 = jnp.bfloat16


def layer_norm(values, gain_row):
    average = jnp.mean(values, axis=-1, keepdims=True)
    centred = values - average
    variance = jnp.mean(centred * centred, axis=-1, keepdims=True)
    return (centred * lax.rsqrt(variance + EPSILON) * gain_row).astype(BF16)


def dot32(left, right):
    return jnp.dot(left, right, preferred_element_type=F32)


def project_queries(normed, weights):
    scale = math.log2(math.e) / math.sqrt(weights.shape[1] // HEADS)
    return (dot32(normed, weights) * scale).astype(BF16)


def attend(units, allowed, head_size, exp_type):
    count, width = units[0][0].shape
    per = LANES // head_size
    head_of_lane = lax.broadcasted_iota(jnp.int32, (count, LANES), 1) // head_size
    both = jnp.concatenate([head_of_lane, head_of_lane], axis=1)
    ones = jnp.ones((units[0][1].shape[0], LANES), BF16)
    groups = width // LANES
    cuts = [slice(group * LANES, (group + 1) * LANES) for group in range(groups)]
    jobs = [[part[:, at] for part in unit] for unit in units for at in cuts]
    scores = []
    for queries, keys, _ in jobs:
        spread = jnp.concatenate(
            [jnp.where(head_of_lane == head, queries, jnp.zeros_like(queries)) for head in range(per)], axis=0
        )
        scores.append(
            lax.dot_general(spread, keys, (((1,), (1,)), ((), ())), preferred_element_type=F32)
        )
    weights = []
    for score in scores:
        score = jnp.where(allowed[None], score.reshape(per, count, -1), -jnp.inf)
        highest = jnp.max(score, axis=-1, keepdims=True)
        weights.append(jnp.exp2((score - highest).astype(exp_type)).astype(BF16).reshape(per * count, -1))
    mixes = [
        dot32(weight, jnp.concatenate([values, ones], axis=1)).reshape(per, count, 2 * LANES)
        for weight, (_, _, values) in zip(weights, jobs)
    ]
    pieces = []
    for mixed in mixes:
        picked = mixed[0]
        for head in range(1, per):
            picked = jnp.where(both == head, mixed[head], picked)
        pieces.append((picked[:, :LANES] / picked[:, LANES:]).astype(BF16))
    return [
        jnp.concatenate(pieces[first : first + groups], axis=1) for first in range(0, len(pieces), groups)
    ]


SHIFT, BOTH_COUNTS, EDGE_COUNTS, FACTS = 0, 1, 5, 16


def fact(facts_ref, row):
    return facts_ref[row : row + 1, :1]


def count_of_row(facts_ref, first, rows):
    wanted = fact(facts_ref, first)
    for row in range(1, WIN_ROWS):
        wanted = jnp.where(rows == row, fact(facts_ref, first + row), wanted)
    return wanted


def edge_block(shifts_ref):
    return jnp.where(shifts_ref[0] == WIN_LON - 1, 0, 1)


def pack_kernel(
    shifts_hbm, counts_hbm, fields_hbm, east_ref, edge_ref, other_ref, facts_ref, shifts_ref, counts_ref, fields_ref,
    sems,
):
    runs, cells, width = edge_ref.shape
    moves = [(shifts_hbm, shifts_ref), (counts_hbm, counts_ref), (fields_hbm, fields_ref)]
    copies = [pltpu.make_async_copy(*ends, sems.at[n]) for n, ends in enumerate(moves)]
    for copy in copies:
        copy.start()
    for copy in copies:
        copy.wait()
    block = edge_block(shifts_ref)
    edge = fields_ref[:, block].reshape(runs, cells, width)
    other = fields_ref[:, 1 - block].reshape(runs, cells, width)
    edge_ref[...] = edge
    other_ref[...] = east_ref[1:] = other
    edge = edge.astype(F32)
    east_ref[0] = jnp.concatenate([edge[run, cells - 1 :] for run in range(runs)], axis=0).astype(BF16)
    numbers = [shifts_ref[1 - block]]
    numbers += [counts_ref[(1 - block) * WIN_ROWS + row] for row in range(WIN_ROWS)]
    numbers += [counts_ref[block * WIN_ROWS + row] for row in range(WIN_ROWS)]
    place = lax.broadcasted_iota(jnp.int32, facts_ref.shape, 0)
    facts = jnp.zeros(facts_ref.shape, jnp.int32)
    for row, number in enumerate(numbers):
        facts = jnp.where(place == row, number, facts)
    facts_ref[...] = facts


def own_kernel(edge_ref, other_ref, gains_ref, qkv_ref, edge_out_ref, other_out_ref):
    total, width = edge_out_ref.shape[1:]
    outs = (edge_out_ref, other_out_ref)
    normed = [
        layer_norm(own[...].reshape(total, width).astype(F32), gains_ref[0:1]) for own in (edge_ref, other_ref)
    ]
    for n in range(3):
        for part, out_ref in zip(normed, outs):
            project = dot32 if n > 0 else project_queries
            out_ref[n] = project(part, qkv_ref[n]).astype(BF16)


def window_block(
    circle, shift, counts_row, other, own, done_ref, facts_ref, anchor_ref, gains_ref, qkv_ref, out_w_ref, result_ref,
    normed_ref,
):
    total, width = own.shape
    tokens = WIN_ROWS * WIN_LON
    anchor = anchor_ref[:1, :1]
    normed = layer_norm(other, gains_ref[0:1])
    keys, values = [dot32(normed, qkv_ref[n]).astype(BF16) for n in (1, 2)]

    shape = (tokens, 2 * tokens)
    query_place = lax.broadcasted_iota(jnp.int32, shape, 0) % WIN_LON
    key = lax.broadcasted_iota(jnp.int32, shape, 1)
    where = key % WIN_LON
    here = key < tokens
    cell = anchor + where
    away = jnp.where(where < shift, cell + WIN_LON, cell - WIN_LON + circle)
    cell = jnp.where(here, cell, jnp.where(away >= circle, away - circle, away))
    same = (query_place < shift) == (where < shift)
    allowed = (here == same) & (cell < count_of_row(facts_ref, counts_row, (key // WIN_LON) % WIN_ROWS))
    units = []
    for first in range(0, total, tokens):
        at = slice(first, first + tokens)
        units.append(
            (
                done_ref[0, at],
                jnp.concatenate([done_ref[1, at], keys[at]], axis=0),
                jnp.concatenate([done_ref[2, at], values[at]], axis=0),
            )
        )
    mixed = jnp.concatenate(attend(units, allowed, width // HEADS, F32), axis=0)
    half = total // 2
    halves = [slice(0, half), slice(half, total)]
    resident = [(own[at] + dot32(mixed[at], out_w_ref[...])).astype(BF16) for at in halves]
    for at, part in zip(halves, resident):
        result_ref[at] = part
        normed_ref[at] = layer_norm(part.astype(F32), gains_ref[1:2])


def window_edge_kernel(
    circle, facts_ref, anchor_ref, own_ref, done_ref, behind_ref, ahead_ref, gains_ref, qkv_ref, out_w_ref, _,
    result_ref, normed_ref,
):
    total, width = result_ref.shape
    cells = behind_ref[0].astype(F32)
    behind = jnp.concatenate(
        [jnp.broadcast_to(cells[n : n + 1], (WIN_LON, width)) for n in range(total // WIN_LON)], axis=0
    )
    place = lax.broadcasted_iota(jnp.int32, (total, width), 0) % WIN_LON
    other = jnp.where(place == WIN_LON - 1, behind, ahead_ref[...].reshape(total, width).astype(F32))
    window_block(
        circle, WIN_LON - 1, EDGE_COUNTS, other, own_ref[...].reshape(total, width).astype(F32), done_ref, facts_ref,
        anchor_ref, gains_ref, qkv_ref, out_w_ref, result_ref, normed_ref,
    )


def window_both_kernel(
    circle, facts_ref, anchor_ref, own_ref, done_ref, behind_ref, ahead_ref, gains_ref, qkv_ref, out_w_ref, result_ref,
    normed_ref,
):
    total, width = result_ref.shape
    shift = fact(facts_ref, SHIFT)
    place = lax.broadcasted_iota(jnp.int32, (total, width), 0) % WIN_LON
    behind = behind_ref[1:].reshape(total, width).astype(F32)
    ahead = ahead_ref[...].reshape(total, width).astype(F32)
    window_block(
        circle, shift, BOTH_COUNTS, jnp.where(place < shift, ahead, behind),
        own_ref[...].reshape(total, width).astype(F32), done_ref, facts_ref, anchor_ref, gains_ref, qkv_ref, out_w_ref,
        result_ref, normed_ref,
    )


def column_attend(queries, keys, values):
    tokens, width = queries.shape
    total = keys.shape[0]
    span = WIN_ROWS * WIN_LON
    levels = tokens // span
    all_levels = total // span
    queries = queries.reshape(levels, WIN_ROWS, WIN_LON, width)
    keys = keys.reshape(all_levels, WIN_ROWS, WIN_LON, width)
    values = values.reshape(all_levels, WIN_ROWS, WIN_LON, width)
    shape = (levels * WIN_LON, all_levels * WIN_LON)
    allowed = (
        lax.broadcasted_iota(jnp.int32, shape, 0) % WIN_LON
        == lax.broadcasted_iota(jnp.int32, shape, 1) % WIN_LON
    )
    mixed = []
    for first in range(0, WIN_ROWS, 2):
        units = [
            (
                queries[:, row].reshape(levels * WIN_LON, width),
                keys[:, row].reshape(all_levels * WIN_LON, width),
                values[:, row].reshape(all_levels * WIN_LON, width),
            )
            for row in (first, first + 1)
        ]
        mixed += attend(units, allowed, width // HEADS, BF16)
    mixed = jnp.concatenate([part.reshape(levels, 1, WIN_LON, width) for part in mixed], axis=1)
    return mixed.reshape(tokens, width)


def feed_forward(mixed, resident_ref, gains_ref, out_w_ref, in_ref, mlp_ref):
    tokens = mixed.shape[0]
    half = tokens // 2
    halves = [slice(0, half), slice(half, tokens)]
    updated = [
        (resident_ref[at].astype(F32) + dot32(mixed[at], out_w_ref[...])).astype(BF16) for at in halves
    ]
    normed = [layer_norm(part.astype(F32), gains_ref[2:3]) for part in updated]
    inner = [dot32(part, in_ref[...]) for part in normed]
    inner = [jax.nn.gelu(part).astype(BF16) for part in inner]
    result = [part.astype(F32) + dot32(act, mlp_ref[...]) for part, act in zip(updated, inner)]
    return jnp.concatenate(result, axis=0)


def live_cells(facts_ref, anchor_ref, counts_row, values):
    tokens = WIN_ROWS * WIN_LON
    width = values.shape[1]
    token = lax.broadcasted_iota(jnp.int32, (tokens, width), 0)
    live = anchor_ref[:1, :1] + token % WIN_LON < count_of_row(facts_ref, counts_row, token // WIN_LON)
    return jnp.where(live[None], values.reshape(-1, tokens, width), 0.0).astype(BF16)


def column_first_kernel(
    facts_ref, anchor_ref, resident_ref, normed_ref, gathered_ref, gains_ref, qkv_ref, out_w_ref, in_ref, mlp_ref,
    result_ref,
):
    queries = project_queries(normed_ref[...], qkv_ref[0])
    gathered = gathered_ref[...].reshape(-1, resident_ref.shape[1])
    keys, values = [dot32(gathered, qkv_ref[n]).astype(BF16) for n in (1, 2)]
    mixed = column_attend(queries, keys, values)
    result = feed_forward(mixed, resident_ref, gains_ref, out_w_ref, in_ref, mlp_ref)
    result_ref[...] = live_cells(facts_ref, anchor_ref, BOTH_COUNTS, result)


def column_own_kernel(normed_ref, qkv_ref, _, result_ref):
    normed = normed_ref[...]
    result_ref[0] = project_queries(normed, qkv_ref[0])
    for n in (1, 2):
        result_ref[n] = dot32(normed, qkv_ref[n]).astype(BF16)


def column_last_kernel(
    core_ref, shifts_hbm, facts_ref, anchor_ref, resident_ref, done_ref, swapped_ref, gathered_ref, first_ref,
    gains_ref, qkv_ref, out_w_ref, in_ref, mlp_ref, result_ref, stage_ref, shifts_ref, sems,
):
    shifts_copy = pltpu.make_async_copy(shifts_hbm, shifts_ref, sems.at[2])
    shifts_copy.start()
    parts, tokens, width = gathered_ref.shape
    half = parts // CORES
    partner = gathered_ref[pl.ds((1 - core_ref[0]) * half, half)].reshape(half * tokens, width)
    rest = jnp.concatenate([swapped_ref[...], partner], axis=0)
    keys, values = [
        jnp.concatenate([done_ref[n], dot32(rest, qkv_ref[n]).astype(BF16)], axis=0) for n in (1, 2)
    ]
    mixed = column_attend(done_ref[0], keys, values)
    shifts_copy.wait()
    block = edge_block(shifts_ref)
    first = pltpu.make_async_copy(first_ref, result_ref.at[:, 1 - block], sems.at[0])
    first.start()
    result = feed_forward(mixed, resident_ref, gains_ref, out_w_ref, in_ref, mlp_ref)
    stage_ref[...] = live_cells(facts_ref, anchor_ref, EDGE_COUNTS, result)
    second = pltpu.make_async_copy(stage_ref, result_ref.at[:, block], sems.at[1])
    second.start()
    first.wait()
    second.wait()


def call(body, outs, scalars, arrays, flops, scratch=(), spaces=None, out_spaces=None):
    spaces = spaces or [pltpu.VMEM] * len(arrays)
    out = [pl.BlockSpec(memory_space=space) for space in out_spaces or [pltpu.VMEM] * len(outs)]
    moved = sum(math.prod(a.shape) * a.dtype.itemsize for a in arrays)
    single = len(outs) == 1
    arrays = [
        pltpu.with_memory_space_constraint(array, space) if space == pltpu.HBM else array
        for array, space in zip(arrays, spaces)
    ]
    return pl.pallas_call(
        body,
        out_shape=outs[0] if single else outs,
        in_specs=[pl.BlockSpec(memory_space=pltpu.SMEM)] * len(scalars)
        + [pl.BlockSpec(memory_space=space) for space in spaces],
        out_specs=out[0] if single else out,
        scratch_shapes=scratch,
        compiler_params=pltpu.CompilerParams(vmem_limit_bytes=24 * 1024 * 1024),
        cost_estimate=pl.CostEstimate(flops=flops, bytes_accessed=moved, transcendentals=0),
    )(*scalars, *arrays)


def local(
    fields,
    counts,
    shifts,
    norm_gains,
    window_qkv,
    window_out,
    column_qkv,
    column_out,
    mlp_in,
    mlp_out,
):
    levels, row_count, cells, width = fields.shape
    blocks = row_count // WIN_ROWS
    tokens = WIN_ROWS * cells
    total = levels * tokens
    runs = levels * WIN_ROWS
    tiles = lax.axis_size("lon")
    circle = cells * tiles
    anchor = jnp.full((8, LANES), lax.axis_index("lon") * cells, jnp.int32)

    weights = [norm_gains, window_qkv, window_out]
    sent, edge, other, facts = call(
        pack_kernel,
        [
            jax.ShapeDtypeStruct((1 + runs, cells, width), BF16),
            jax.ShapeDtypeStruct((runs, cells, width), BF16),
            jax.ShapeDtypeStruct((runs, cells, width), BF16),
            jax.ShapeDtypeStruct((FACTS, LANES), jnp.int32),
        ],
        [],
        [shifts, counts, fields.reshape(levels, blocks, WIN_ROWS, cells, width)],
        10**10,
        [
            pltpu.SMEM(shifts.shape, jnp.int32),
            pltpu.SMEM(counts.shape, jnp.int32),
            pltpu.VMEM((levels, blocks, WIN_ROWS, cells, width), BF16),
            pltpu.SemaphoreType.DMA((6,)),
        ],
        [pltpu.HBM] * 3,
    )
    west = [(tile, (tile - 1) % tiles) for tile in range(tiles)]
    behind = lax.ppermute(sent, "lon", [pair[::-1] for pair in west])
    ahead_other = lax.ppermute(other, "lon", west)

    one = jax.ShapeDtypeStruct((total, width), BF16)
    three = jax.ShapeDtypeStruct((3, total, width), BF16)
    done_edge, done_other = call(own_kernel, [three, three], [], [edge, other] + weights[:2], 10**9)
    ahead_edge = lax.ppermute(edge, "lon", west)
    resident_other, normed_other = call(
        functools.partial(window_both_kernel, circle),
        [one, one],
        [],
        [facts, anchor, other, done_other, behind, ahead_other] + weights,
        10**9,
    )
    resident_edge, normed_edge = call(
        functools.partial(window_edge_kernel, circle),
        [one, one],
        [],
        [facts, anchor, edge, done_edge, behind, ahead_edge] + weights + [resident_other],
        10**9,
        spaces=[pltpu.VMEM] * (6 + len(weights)) + [pl.ANY],
    )

    groups = [[first, first + 1] for first in range(0, 2 * CORES, CORES)]
    swap = [(n, n ^ CORES) for n in range(2 * CORES)]

    def gather(part, other):
        return lax.all_gather(jnp.stack([part, other]), "lev", tiled=True, axis_index_groups=groups)

    swapped_other, swapped_edge = [lax.ppermute(part, "lev", swap) for part in (normed_other, normed_edge)]
    weights = [norm_gains, column_qkv, column_out, mlp_in, mlp_out]
    first = call(
        column_first_kernel,
        [jax.ShapeDtypeStruct((levels, tokens, width), BF16)],
        [],
        [facts, anchor, resident_other, normed_other, gather(normed_other, swapped_other)] + weights,
        10**9,
    )
    done = call(
        column_own_kernel,
        [three],
        [],
        [normed_edge, column_qkv, first],
        10**9,
        spaces=[pltpu.VMEM, pltpu.VMEM, pl.ANY],
    )
    first, swapped_edge = lax.optimization_barrier((first, swapped_edge))
    core = (lax.axis_index("lev") % CORES).astype(jnp.int32).reshape(1)
    result = call(
        column_last_kernel,
        [jax.ShapeDtypeStruct((levels, blocks, tokens, width), BF16)],
        [core],
        [shifts, facts, anchor, resident_edge, done, swapped_edge, gather(normed_edge, swapped_edge), first] + weights,
        10**9,
        [
            pltpu.VMEM((levels, tokens, width), BF16),
            pltpu.SMEM(shifts.shape, jnp.int32),
            pltpu.SemaphoreType.DMA((3,)),
        ],
        [pltpu.HBM] + [pltpu.VMEM] * (7 + len(weights)),
        out_spaces=[pltpu.HBM],
    )
    return result.reshape(fields.shape)


def solution(mesh):
    return jax.shard_map(
        local,
        mesh=mesh,
        in_specs=(P("lev", None, "lon", None), P(), P(), P(), P(), P(), P(), P(), P(), P()),
        out_specs=P("lev", None, "lon", None),
        check_vma=False,
    )
```
